32 devices in a mesh: seq: 16 (over z, x, core), tp: 2 (over y).
Axes of the slice: x: 2, y: 2, z: 4, core: 2. Of those that a mesh axis runs over, the one named last changes fastest.
Arguments:
- hidden: bfloat16 [2048, 3072], P('seq'), may hold values from -6 to 6
- latent: float32 [2048, 64], P('seq'), may hold values from -6 to 6
- key_cache: bfloat16 [2048, 2048], P('seq', 'tp'), may hold values from -8 to 8
- value_cache: bfloat16 [2048, 2048], P('seq', 'tp'), may hold values from -6 to 6
- text_keys: bfloat16 [4, 512, 2048], P(None, None, 'tp'), may hold values from -128 to 128
- text_values: bfloat16 [4, 512, 2048], P(None, None, 'tp'), may hold values from -6 to 6
- query_weight: bfloat16 [3072, 2048], P('seq', 'tp'), may hold values from -0.109375 to 0.109375
- key_weight: bfloat16 [3072, 2048], P('seq', 'tp'), may hold values from -0.109375 to 0.109375
- value_weight: bfloat16 [3072, 2048], P('seq', 'tp'), may hold values from -0.109375 to 0.109375
- out_weight: bfloat16 [3072, 2048], P('seq', 'tp'), may hold values from -0.1875 to 0.1875
- query_gain: float32 [128], replicated, may hold values from 1.2 to 2.5
- key_gain: float32 [128], replicated, may hold values from 1.2 to 2.5
- mod_shift: float32 [4, 3072], replicated, may hold values from -3 to 3
- mod_scale: float32 [4, 3072], replicated, may hold values from -0.9 to 0.9
- mod_gate: float32 [4, 3072], replicated, may hold values from -4 to 4
- final_weight: bfloat16 [3072, 64], P('tp'), may hold values from -0.109375 to 0.109375
- conv_weight: bfloat16 [144, 512], P(None, 'tp'), may hold values from -0.5 to 0.5
- image_rows: int32 [4], replicated, may hold values from 1 to 24, as said below
- tile_owner: int32 [16], replicated, may hold values from 0 to 4, as said below
- listed: int32 [16, 32], P('seq'), may hold values from 0 to 127, as said below
- step_index: int32 [4], replicated, may hold values from 0 to 7
Outputs:
- hidden_next: bfloat16 [2048, 3072], P('seq', 'tp')
- latent_next: float32 [2048, 64], P('seq')
- decoded: bfloat16 [8192, 512], P('seq', 'tp')
The draws below stay inside these ranges and needn't reach their ends.
Inputs may be any that keep to these rules, and one draw needn't show every extreme that they name: `image_rows`: one request has exactly 24 rows. `tile_owner`: the tiles of each request are consecutive and in request order, a request of r rows holds ceil(r * 64 / 128) tiles, and every tile after them holds 4, meaning no request. The rows listed for one tile are distinct.
All inputs are finite; a program needn't handle non-finite values.
Results may differ from the reference program's by a relative error of at most 0.009.
Values may be sent and summed in bfloat16 or wider, within the bound.
A program may use at most 64 MiB of HBM per device.

```python
import math
import jax
import jax.numpy as jnp
from jax import lax

D = 3072
HEADS = 16
HD = 128
LAT_CH = 64
OUTCH = 512
IMG_W = 64
TEXT = 512
REQS = 4
STEPS = 8
TILE = 128
TOKENS = 2048
N_SEQ = 16


def layout_draw(key):
    largest_key, tiles_key, rows_key = jax.random.split(jax.random.fold_in(key, 7), 3)
    largest = jax.random.randint(largest_key, (), 0, REQS)
    big_tiles = 3 * N_SEQ // 4
    token_rows = TILE // IMG_W
    other_most = (N_SEQ - big_tiles) // (REQS - 1)
    tile_share = jax.random.randint(tiles_key, (REQS,), 1, other_most + 1)
    tile_share = jnp.where(jnp.arange(REQS) == largest, big_tiles, tile_share)
    last_rows = jax.random.randint(rows_key, (REQS,), 1, token_rows + 1)
    row_counts = (tile_share - 1) * token_rows + last_rows
    row_counts = jnp.where(jnp.arange(REQS) == largest, big_tiles * token_rows, row_counts)
    tile_ends = jnp.cumsum(tile_share)
    owners = jnp.sum((jnp.arange(N_SEQ)[:, None] >= tile_ends[None, :]).astype(jnp.int32), axis=1)
    return (row_counts.astype(jnp.int32), owners.astype(jnp.int32))


def draw_image_rows(key, part):
    return layout_draw(key)[0]


def draw_tile_owner(key, part):
    return layout_draw(key)[1]


def draw_listed(key, part):
    tile_keys = jax.random.split(jax.random.fold_in(key, 11), N_SEQ)
    orders = jax.vmap(lambda one_key: jax.random.permutation(one_key, TILE))(tile_keys)
    return orders[:, :TILE // 4].astype(jnp.int32)


def draw_text_keys(key, part):
    base_key = jax.random.fold_in(jax.random.fold_in(key, 23), 0)
    sample = jax.random.normal(base_key, (REQS, TEXT, HEADS * HD), jnp.float32)
    return jnp.clip(sample, -128.0, 128.0).astype(jnp.bfloat16)


def with_ends(drawn, stream_key, least, high):
    longest = drawn.shape.index(max(drawn.shape))
    spots = []
    for shift in (0, 1):
        where = [jax.random.randint(jax.random.fold_in(stream_key, axis), (), 0, length) for axis, length in enumerate(drawn.shape)]
        where[longest] = (where[longest] + shift) % drawn.shape[longest]
        spots.append(tuple(where))
    return drawn.at[spots[0]].set(least).at[spots[1]].set(high)


def strengthened(values, own_key, source, target, blocks, factor):
    def block_of(position):
        return (jnp.arange(values.shape[position]) // (values.shape[position] // blocks)).reshape((-1,) + (1,) * (values.ndim - 1 - position))

    near = jax.random.permutation(own_key, blocks)[block_of(target)]
    other_side = (block_of(target) + blocks // 2) % blocks
    return jnp.where((block_of(source) == near) | (block_of(source) == other_side), factor * values, values)


def shard_levels(stream_key, extent, cuts, smallest, high):
    factor_of, own = 1.0, jax.random.fold_in(stream_key, 6)
    for position, shards_of in cuts:
        steps = jnp.exp(jax.random.uniform(jax.random.fold_in(own, position), (shards_of,), jnp.float32, smallest / len(cuts), high / len(cuts)))
        factor_of = factor_of * jnp.repeat(steps, extent[position] // shards_of).reshape([-1 if axis == position else 1 for axis in range(len(extent))])
    return factor_of


def gaussian(own_key, shape, width, limit, pieces=(), held_as=jnp.bfloat16):
    array = jax.random.normal(own_key, shape, jnp.float32) * width
    if len(pieces) > 0:
        array = shard_levels(own_key, shape, pieces, -0.22, 0.18) * array
    return jnp.clip(array, min=-limit, max=limit).astype(held_as)


def gaussian_with(own_key, shape, scale, bound, cuts, heavy, kind=jnp.bfloat16):
    values = scale * jax.random.normal(own_key, shape, jnp.float32)
    if cuts:
        values = values * shard_levels(own_key, shape, cuts, -0.22, 0.18)
    return jnp.clip(strengthened(values, jax.random.fold_in(own_key, 3), *heavy), -bound, bound).astype(kind)


def setup_inputs(seed: int = 0) -> dict:
    key_list = jax.random.split(jax.random.key(seed), 22)
    hidden = gaussian(key_list[0], (TOKENS, D), 1.0, 6.0, ((0, 16),))
    latent = gaussian(key_list[1], (TOKENS, LAT_CH), 1.0, 6.0, ((0, 16),), jnp.float32)
    key_cache = gaussian(key_list[2], (TOKENS, HEADS * HD), 1.5, 8.0, ((0, 16), (1, 2)))
    value_cache = gaussian(key_list[3], (TOKENS, HEADS * HD), 1.0, 6.0, ((0, 16), (1, 2)))
    text_keys = draw_text_keys(jax.random.fold_in(key_list[21], 71), 0)
    text_values = gaussian(key_list[5], (REQS, TEXT, HEADS * HD), 1.0, 6.0, ((2, 2),))
    query_weight = gaussian(key_list[6], (D, HEADS * HD), D ** -0.5, 0.109375, ((0, 16), (1, 2)))
    key_weight = gaussian(key_list[7], (D, HEADS * HD), D ** -0.5, 0.109375, ((0, 16), (1, 2)))
    value_weight = gaussian(key_list[8], (D, HEADS * HD), D ** -0.5, 0.109375, ((0, 16), (1, 2)))
    out_weight = gaussian_with(key_list[9], (D, HEADS * HD), (HEADS * HD) ** -0.5, 0.1875, ((0, 16), (1, 2)), (1, 0, 16, 2.0))
    query_gain = jnp.clip(jnp.exp(jax.random.uniform(key_list[10], (HD,), jnp.float32, math.log(1.2), math.log(2.5))), 1.2, 2.5)
    key_gain = jnp.clip(jnp.exp(jax.random.uniform(key_list[11], (HD,), jnp.float32, math.log(1.2), math.log(2.5))), 1.2, 2.5)
    mod_shift = gaussian(key_list[12], (REQS, D), 0.5, 3.0, (), jnp.float32)
    mod_scale = gaussian(key_list[13], (REQS, D), 0.3, 0.9, (), jnp.float32)
    mod_gate = gaussian(key_list[14], (REQS, D), 1.0, 4.0, (), jnp.float32)
    final_weight = gaussian(key_list[15], (D, LAT_CH), D ** -0.5, 0.109375, ((0, 2),))
    conv_weight = gaussian(key_list[16], (9 * (LAT_CH // 4), OUTCH), (9 * (LAT_CH // 4)) ** -0.5, 0.5, ((1, 2),))
    image_rows = draw_image_rows(jax.random.fold_in(key_list[21], 71), 0)
    tile_owner = draw_tile_owner(jax.random.fold_in(key_list[21], 71), 0)
    listed = draw_listed(jax.random.fold_in(key_list[21], 71), 0)
    step_index = with_ends(jax.random.randint(key_list[20], (REQS,), 0, STEPS), jax.random.fold_in(key_list[20], 1), 0, STEPS - 1).astype(jnp.int32)
    return dict(hidden=hidden, latent=latent, key_cache=key_cache, value_cache=value_cache, text_keys=text_keys, text_values=text_values, query_weight=query_weight, key_weight=key_weight, value_weight=value_weight, out_weight=out_weight, query_gain=query_gain, key_gain=key_gain, mod_shift=mod_shift, mod_scale=mod_scale, mod_gate=mod_gate, final_weight=final_weight, conv_weight=conv_weight, image_rows=image_rows, tile_owner=tile_owner, listed=listed, step_index=step_index)


EPSILON = 1e-06
SIGMA_SHIFT = 3.0

def tile_layout(tile_owner, image_rows, tile_rows, row_width):
    request_count = image_rows.shape[0]
    tile_count = tile_owner.shape[0]
    earlier = lax.optimization_barrier(jnp.sum((tile_owner[None, :] < tile_owner[:, None]).astype(jnp.int32), axis=1))
    ordinal = jnp.arange(tile_count, dtype=jnp.int32) - earlier
    mod_req = jnp.minimum(tile_owner, request_count - 1)
    picked = lax.optimization_barrier(jnp.sum(jnp.where(mod_req[:, None] == jnp.arange(request_count, dtype=jnp.int32)[None, :], image_rows[None, :], 0), axis=1))
    live_rows = jnp.where(tile_owner < request_count, jnp.clip(picked * row_width - ordinal * tile_rows, 0, tile_rows), 0)
    return (mod_req, live_rows)

def sigma_of(step_index):
    fraction = 1.0 - step_index.astype(jnp.float32) / STEPS
    return SIGMA_SHIFT * fraction / (1.0 + (SIGMA_SHIFT - 1.0) * fraction)

def head_norm(projected, head_gain):
    row_count = projected.shape[0]
    shaped = projected.reshape(row_count, -1, HD)
    inverse = lax.rsqrt(lax.optimization_barrier(jnp.mean(jnp.square(shaped), axis=2, keepdims=True)) + EPSILON)
    return shaped * inverse * head_gain

def reference(hidden, latent, key_cache, value_cache, text_keys, text_values, query_weight, key_weight, value_weight, out_weight, query_gain, key_gain, mod_shift, mod_scale, mod_gate, final_weight, conv_weight, image_rows, tile_owner, listed, step_index):
    tile_count = tile_owner.shape[0]
    tile_rows = hidden.shape[0] // tile_count
    mod_req, live_rows = tile_layout(tile_owner, image_rows, tile_rows, IMG_W)
    row_index = jnp.arange(tile_rows, dtype=jnp.int32)
    token_req = jnp.where(row_index[None, :] < live_rows[:, None], tile_owner[:, None], -1).reshape(-1)
    token_mod = jnp.repeat(mod_req, tile_rows)
    hidden_f32 = hidden.astype(jnp.float32)
    row_mean = lax.optimization_barrier(jnp.mean(hidden_f32, axis=1, keepdims=True))
    row_var = lax.optimization_barrier(jnp.mean(jnp.square(hidden_f32 - row_mean), axis=1, keepdims=True))
    normed = (hidden_f32 - row_mean) * lax.rsqrt(row_var + EPSILON)
    modulated = ((1.0 + mod_scale[token_mod]) * normed + mod_shift[token_mod]).astype(jnp.bfloat16)
    queries = head_norm(jnp.dot(modulated, query_weight, preferred_element_type=jnp.float32), query_gain).astype(jnp.bfloat16)
    listed_global = (jnp.arange(tile_count, dtype=jnp.int32)[:, None] * tile_rows + listed).reshape(-1)
    listed_x = modulated[listed_global]
    fresh_keys = head_norm(jnp.dot(listed_x, key_weight, preferred_element_type=jnp.float32), key_gain).astype(jnp.bfloat16).reshape(-1, HEADS * HD)
    fresh_values = jnp.dot(listed_x, value_weight, preferred_element_type=jnp.float32).astype(jnp.bfloat16)
    all_keys = key_cache.at[listed_global].set(fresh_keys).astype(jnp.float32).reshape(-1, HEADS, HD)
    all_values = value_cache.at[listed_global].set(fresh_values).astype(jnp.float32).reshape(-1, HEADS, HD)
    score_scale = 1.0 / math.sqrt(HD)

    def one_tile(tile_id):
        tile_q = lax.dynamic_slice_in_dim(queries, tile_id * tile_rows, tile_rows, 0).astype(jnp.float32)
        own_req = lax.dynamic_slice_in_dim(token_req, tile_id * tile_rows, tile_rows, 0)
        request = mod_req[tile_id]
        text_key_tile = lax.dynamic_index_in_dim(text_keys, request, 0, keepdims=False).astype(jnp.float32).reshape(TEXT, HEADS, HD)
        text_value_tile = lax.dynamic_index_in_dim(text_values, request, 0, keepdims=False).astype(jnp.float32).reshape(TEXT, HEADS, HD)
        text_scores = jnp.einsum('qhd,khd->hqk', tile_q, text_key_tile) * score_scale
        image_scores = jnp.einsum('qhd,khd->hqk', tile_q, all_keys) * score_scale
        allowed = (token_req[None, :] == own_req[:, None]) & (own_req[:, None] >= 0)
        image_scores = jnp.where(allowed[None], image_scores, -jnp.inf)
        row_max = jnp.maximum(lax.optimization_barrier(jnp.max(text_scores, axis=2)), lax.optimization_barrier(jnp.max(image_scores, axis=2)))
        text_exp = jnp.exp(text_scores - row_max[..., None])
        image_exp = jnp.exp(image_scores - row_max[..., None])
        row_sum = lax.optimization_barrier(jnp.sum(text_exp, axis=2)) + lax.optimization_barrier(jnp.sum(image_exp, axis=2))
        weighted = jnp.einsum('hqk,khd->hqd', text_exp.astype(jnp.bfloat16).astype(jnp.float32), text_value_tile)
        weighted = weighted + jnp.einsum('hqk,khd->hqd', image_exp.astype(jnp.bfloat16).astype(jnp.float32), all_values)
        result = weighted / row_sum[..., None]
        return jnp.transpose(result, (1, 0, 2)).reshape(tile_rows, HEADS * HD).astype(jnp.bfloat16)
    attended = lax.map(one_tile, jnp.arange(tile_count, dtype=jnp.int32)).reshape(-1, HEADS * HD)
    projected = lax.dot_general(attended, out_weight, (((1,), (1,)), ((), ())), preferred_element_type=jnp.float32)
    hidden_next = (hidden_f32 + mod_gate[token_mod] * projected).astype(jnp.bfloat16)
    velocity = jnp.dot(hidden_next, final_weight, preferred_element_type=jnp.float32)
    step_delta = sigma_of(step_index + 1) - sigma_of(step_index)
    latent_next = latent + step_delta[token_mod][:, None] * velocity
    token_live = token_req >= 0
    dec_input = jnp.where(token_live[:, None], latent_next, 0.0).astype(jnp.bfloat16)
    token_rows = tile_rows // IMG_W
    pixel_ch = LAT_CH // 4
    pixels = dec_input.reshape(tile_count, token_rows, IMG_W, pixel_ch, 2, 2)
    pixels = jnp.transpose(pixels, (0, 1, 4, 2, 5, 3)).reshape(tile_count, 2 * token_rows, 2 * IMG_W, pixel_ch)
    same_prev = jnp.concatenate([jnp.zeros((1,), dtype=bool), tile_owner[1:] == tile_owner[:-1]])
    same_next = jnp.concatenate([tile_owner[:-1] == tile_owner[1:], jnp.zeros((1,), dtype=bool)])
    prev_row = jnp.where(same_prev[:, None, None], jnp.roll(pixels[:, -1], 1, axis=0), 0.0).astype(jnp.bfloat16)
    next_row = jnp.where(same_next[:, None, None], jnp.roll(pixels[:, 0], -1, axis=0), 0.0).astype(jnp.bfloat16)
    framed = jnp.concatenate([prev_row[:, None], pixels, next_row[:, None]], axis=1)
    framed = jnp.pad(framed, ((0, 0), (0, 0), (1, 1), (0, 0)))
    patches = jnp.concatenate([framed[:, row_shift:row_shift + 2 * token_rows, col_shift:col_shift + 2 * IMG_W, :] for row_shift in range(3) for col_shift in range(3)], axis=-1)
    convolved = jnp.dot(patches.reshape(-1, 9 * pixel_ch), conv_weight, preferred_element_type=jnp.float32)
    pixel_live = jnp.broadcast_to(token_live.reshape(tile_count, token_rows, 1, IMG_W, 1), (tile_count, token_rows, 2, IMG_W, 2)).reshape(-1)
    decoded = jnp.where(pixel_live[:, None], convolved, 0.0).astype(jnp.bfloat16)
    return (hidden_next, latent_next, decoded)
```

```python
import math

import jax
import jax.numpy as jnp
from jax import lax
from jax.experimental import pallas as pl
from jax.experimental.pallas import tpu as pltpu
from jax.sharding import PartitionSpec as P

HD = 128
LAT_CH = 64
IMG_W = 64
STEPS = 8


EPSILON = 1e-06
SIGMA_SHIFT = 3.0


def with_halo(shard, sides, width):
    for axis, dim in sides:
        devices, length = (lax.axis_size(axis), shard.shape[dim])
        up = [(i, (i + 1) % devices) for i in range(devices - 1)]
        down = [(j, i) for i, j in up]
        last = lax.slice_in_dim(shard, length - width, length, axis=dim)
        first = lax.slice_in_dim(shard, 0, width, axis=dim)
        before = lax.ppermute(last, axis, up)
        after = lax.ppermute(first, axis, down)
        shard = jnp.concatenate([before, shard, after], axis=dim)
    return shard


def tile_layout(tile_owner, image_rows, tile_rows, row_width):
    request_count = image_rows.shape[0]
    tile_count = tile_owner.shape[0]
    earlier = jnp.sum((tile_owner[None, :] < tile_owner[:, None]).astype(jnp.int32), axis=1)
    ordinal = jnp.arange(tile_count, dtype=jnp.int32) - earlier
    mod_req = jnp.minimum(tile_owner, request_count - 1)
    picked = jnp.sum(
        jnp.where(
            mod_req[:, None] == jnp.arange(request_count, dtype=jnp.int32)[None, :],
            image_rows[None, :],
            0,
        ),
        axis=1,
    )
    live_rows = jnp.where(
        tile_owner < request_count,
        jnp.clip(picked * row_width - ordinal * tile_rows, 0, tile_rows),
        0,
    )
    return (mod_req, live_rows)


def sigma_of(step_index):
    fraction = 1.0 - step_index.astype(jnp.float32) / STEPS
    return SIGMA_SHIFT * fraction / (1.0 + (SIGMA_SHIFT - 1.0) * fraction)


def head_norm(projected, head_gain):
    row_count = projected.shape[0]
    shaped = projected.reshape(row_count, -1, HD)
    inverse = lax.rsqrt(jnp.mean(jnp.square(shaped), axis=2, keepdims=True) + EPSILON)
    return shaped * inverse * head_gain


def plain_branch(
    modulated, listed_rows, key_cache, value_cache, text_keys, text_values,
    query_weight, key_weight, value_weight, out_weight, query_gain, key_gain,
    token_req, own_tokens, own_request,
):
    tile_rows = modulated.shape[0]
    listed_x = modulated[listed_rows]
    local_width = key_cache.shape[1]
    local_heads = local_width // HD
    gathered_q, gathered_k, gathered_v, gathered_out = (
        lax.all_gather(query_weight, "seq", axis=0, tiled=True),
        lax.all_gather(key_weight, "seq", axis=0, tiled=True),
        lax.all_gather(value_weight, "seq", axis=0, tiled=True),
        lax.all_gather(out_weight, "seq", axis=0, tiled=True),
    )
    query_raw = jnp.dot(modulated, gathered_q, preferred_element_type=jnp.float32)
    key_raw = jnp.dot(listed_x, gathered_k, preferred_element_type=jnp.float32)
    value_raw = jnp.dot(listed_x, gathered_v, preferred_element_type=jnp.float32)
    queries = head_norm(query_raw, query_gain).astype(jnp.bfloat16)
    fresh_keys = head_norm(key_raw, key_gain).astype(jnp.bfloat16).reshape(-1, local_width)
    fresh_values = value_raw.astype(jnp.bfloat16)
    local_keys = key_cache.at[listed_rows].set(fresh_keys)
    local_values = value_cache.at[listed_rows].set(fresh_values)
    score_scale = 1.0 / math.sqrt(HD)
    text_key_tile = lax.dynamic_index_in_dim(text_keys, own_request, 0, keepdims=False).reshape(
        -1, local_heads, HD
    )
    text_value_tile = lax.dynamic_index_in_dim(text_values, own_request, 0, keepdims=False).reshape(
        -1, local_heads, HD
    )
    text_scores = (
        jnp.einsum("qhd,khd->hqk", queries, text_key_tile, preferred_element_type=jnp.float32)
        * score_scale
    )
    row_max = jnp.max(text_scores, axis=2)
    text_exp = jnp.exp(text_scores - row_max[..., None])
    row_sum = jnp.sum(text_exp, axis=2)
    weighted = jnp.einsum(
        "hqk,khd->hqd",
        text_exp.astype(jnp.bfloat16),
        text_value_tile,
        preferred_element_type=jnp.float32,
    )

    def attend(state_now, key_tile, value_tile, key_owner):
        old_max, old_sum, old_weighted = state_now
        allowed = (key_owner[None, :] == own_tokens[:, None]) & (own_tokens[:, None] >= 0)
        key_heads = key_tile.reshape(-1, local_heads, HD)
        value_heads = value_tile.reshape(-1, local_heads, HD)
        scores = (
            jnp.einsum("qhd,khd->hqk", queries, key_heads, preferred_element_type=jnp.float32)
            * score_scale
        )
        scores = jnp.where(allowed[None], scores, -jnp.inf)
        new_max = jnp.maximum(old_max, jnp.max(scores, axis=2))
        shrink = jnp.exp(old_max - new_max)
        exp_scores = jnp.exp(scores - new_max[..., None])
        new_sum = old_sum * shrink + jnp.sum(exp_scores, axis=2)
        new_weighted = old_weighted * shrink[..., None] + jnp.einsum(
            "hqk,khd->hqd",
            exp_scores.astype(jnp.bfloat16),
            value_heads,
            preferred_element_type=jnp.float32,
        )
        return (new_max, new_sum, new_weighted)

    pieces = (
        lax.all_gather(local_keys, "seq", axis=0, tiled=True),
        lax.all_gather(local_values, "seq", axis=0, tiled=True),
    )
    length = pieces[0].shape[0]
    key_owner = token_req
    key_block = 1024
    block_count = length // key_block
    stacked = (
        pieces[0].reshape(block_count, key_block, -1),
        pieces[1].reshape(block_count, key_block, -1),
        key_owner.reshape(block_count, key_block),
    )

    def scan_step(state_mid, blocks):
        return (attend(state_mid, blocks[0], blocks[1], blocks[2]), None)

    row_max, row_sum, weighted = lax.scan(scan_step, (row_max, row_sum, weighted), stacked)[0]
    attended = (
        jnp.transpose(weighted / row_sum[..., None], (1, 0, 2))
        .reshape(tile_rows, local_width)
        .astype(jnp.bfloat16)
    )
    partial_out = lax.dot_general(
        attended, gathered_out, (((1,), (1,)), ((), ())), preferred_element_type=jnp.float32
    )
    reduced = lax.psum_scatter(
        partial_out.astype(jnp.bfloat16), "tp", scatter_dimension=1, tiled=True
    ).astype(jnp.float32)
    return reduced


GROUP = 4


def group_size(seq_count, local_heads):
    if seq_count % GROUP == 0 and local_heads % GROUP == 0 and seq_count // GROUP == 4:
        return GROUP
    return 1


def attention_kernel(
    request_ref, place_ref, q_ref, k_ref, v_ref, tk_ref, tv_ref, key_req_ref, tok_req_ref, o_ref
):
    scale = 1.0 / math.sqrt(HD)
    q = q_ref[...]
    dims = (((1,), (1,)), ((), ()))
    s_text = lax.dot_general(q, tk_ref[0], dims, preferred_element_type=jnp.float32) * scale
    s_img = lax.dot_general(q, k_ref[...], dims, preferred_element_type=jnp.float32) * scale
    own = tok_req_ref[...]
    allowed = (key_req_ref[...] == own) & (own >= 0)
    s_img = jnp.where(allowed, s_img, -jnp.inf)
    top = jnp.maximum(
        jnp.max(s_text, axis=1, keepdims=True), jnp.max(s_img, axis=1, keepdims=True)
    )
    e_text = jnp.exp(s_text - top)
    e_img = jnp.exp(s_img - top)
    total = jnp.sum(e_text, axis=1, keepdims=True) + jnp.sum(e_img, axis=1, keepdims=True)
    acc = jnp.dot(e_text.astype(jnp.bfloat16), tv_ref[0], preferred_element_type=jnp.float32)
    acc += jnp.dot(e_img.astype(jnp.bfloat16), v_ref[...], preferred_element_type=jnp.float32)
    o_ref[...] = (acc / total).astype(jnp.bfloat16)


def attention(queries, keys, values, text_keys, text_values, requests, place, token_req, own_req):
    rows, width = queries.shape
    length = keys.shape[0]
    text = text_keys.shape[1]
    heads = width // HD
    tiles = requests.shape[0]
    tile_rows = rows // tiles
    grid_spec = pltpu.PrefetchScalarGridSpec(
        num_scalar_prefetch=2,
        grid=(heads, tiles),
        in_specs=[
            pl.BlockSpec((tile_rows, HD), lambda h, t, req, pos: (t, h)),
            pl.BlockSpec((length, HD), lambda h, t, req, pos: (0, h)),
            pl.BlockSpec((length, HD), lambda h, t, req, pos: (0, h)),
            pl.BlockSpec((1, text, HD), lambda h, t, req, pos: (req[t], 0, pos[0] * heads + h)),
            pl.BlockSpec((1, text, HD), lambda h, t, req, pos: (req[t], 0, pos[0] * heads + h)),
            pl.BlockSpec((1, length), lambda h, t, req, pos: (0, 0)),
            pl.BlockSpec((tile_rows, 1), lambda h, t, req, pos: (t, 0)),
        ],
        out_specs=pl.BlockSpec((tile_rows, HD), lambda h, t, req, pos: (t, h)),
    )
    return pl.pallas_call(
        attention_kernel,
        grid_spec=grid_spec,
        out_shape=jax.ShapeDtypeStruct((rows, width), jnp.bfloat16),
        compiler_params=pltpu.CompilerParams(vmem_limit_bytes=32 * 1024 * 1024),
        cost_estimate=pl.CostEstimate(
            flops=4 * rows * width * (length + text),
            bytes_accessed=8 * length * width,
            transcendentals=rows * heads * (length + text),
        ),
    )(
        requests, place, queries, keys, values, text_keys, text_values,
        token_req.reshape(1, -1), own_req.reshape(-1, 1),
    )


def grouped_branch(
    group, modulated, listed_rows, key_cache, value_cache, text_keys, text_values,
    query_weight, key_weight, value_weight, out_weight, query_gain, key_gain,
    token_req, mod_req,
):
    tile_rows, model = modulated.shape
    seq_count = lax.axis_size("seq")
    seq_index = lax.axis_index("seq")
    lines = seq_count // group
    place = lax.rem(seq_index, group)
    first_tile = seq_index - place
    width = key_cache.shape[1] // group
    depth = query_weight.shape[0]
    inner = [[z * group + p for p in range(group)] for z in range(lines)]
    outer = [[z * group + p for z in range(lines)] for p in range(group)]

    def spread(block):
        return lax.all_to_all(
            block, "seq", split_axis=1, concat_axis=0, axis_index_groups=inner, tiled=True
        )

    def line_gather(block):
        return lax.all_gather(block, "seq", axis=0, axis_index_groups=outer, tiled=True)

    row_index = jnp.arange(tile_rows, dtype=jnp.int32)
    is_listed = jnp.any(row_index[:, None] == listed_rows[None, :], axis=1)
    flagged = jnp.concatenate(
        [
            modulated,
            jnp.broadcast_to(is_listed[:, None], (tile_rows, HD)).astype(jnp.bfloat16),
        ],
        axis=1,
    )
    everyone = lax.all_gather(flagged, "seq", axis=0, axis_index_groups=inner, tiled=True)
    tokens = everyone[:, :model]
    fresh = everyone[:, model : model + 1] > 0
    key_w = line_gather(spread(key_weight))
    value_w = line_gather(spread(value_weight))
    query_w = line_gather(spread(query_weight))
    key_tiles = spread(key_cache)
    value_tiles = spread(value_cache)
    key_raw = jnp.dot(tokens, key_w, preferred_element_type=jnp.float32)
    fresh_keys = head_norm(key_raw, key_gain).astype(jnp.bfloat16).reshape(-1, width)
    keys = line_gather(jnp.where(fresh, fresh_keys, key_tiles))
    value_raw = jnp.dot(tokens, value_w, preferred_element_type=jnp.float32)
    values = line_gather(jnp.where(fresh, value_raw.astype(jnp.bfloat16), value_tiles))
    query_raw = jnp.dot(tokens, query_w, preferred_element_type=jnp.float32)
    queries = head_norm(query_raw, query_gain).astype(jnp.bfloat16).reshape(-1, width)
    out_w = line_gather(out_weight)
    requests = lax.dynamic_slice_in_dim(mod_req, first_tile, group)
    own_req = lax.dynamic_slice_in_dim(token_req, first_tile * tile_rows, group * tile_rows)
    attended = attention(
        queries, keys, values, text_keys, text_values, requests, place.reshape(1),
        token_req, own_req,
    )
    attended = lax.all_gather(attended, "seq", axis=1, axis_index_groups=inner, tiled=True)
    partial_out = lax.dot_general(
        attended, out_w, (((1,), (1,)), ((), ())), preferred_element_type=jnp.float32
    )
    halves = lax.psum_scatter(
        partial_out.astype(jnp.bfloat16), "tp", scatter_dimension=1, tiled=True
    )
    own = lax.all_to_all(
        halves.reshape(group, tile_rows, -1), "seq", split_axis=0, concat_axis=0,
        axis_index_groups=inner, tiled=True,
    )
    own = own.reshape(group, tile_rows, -1, depth)
    return jnp.transpose(own, (1, 2, 0, 3)).reshape(tile_rows, -1).astype(jnp.float32)


def shards(
    hidden,
    latent,
    key_cache,
    value_cache,
    text_keys,
    text_values,
    query_weight,
    key_weight,
    value_weight,
    out_weight,
    query_gain,
    key_gain,
    mod_shift,
    mod_scale,
    mod_gate,
    final_weight,
    conv_weight,
    image_rows,
    tile_owner,
    listed,
    step_index,
):
    tile_rows = hidden.shape[0]
    seq_count = lax.axis_size("seq")
    seq_index = lax.axis_index("seq")
    tp_index = lax.axis_index("tp")
    request_count = image_rows.shape[0]
    mod_req, live_rows = tile_layout(tile_owner, image_rows, tile_rows, IMG_W)
    row_index = jnp.arange(tile_rows, dtype=jnp.int32)
    token_req = jnp.where(row_index[None, :] < live_rows[:, None], tile_owner[:, None], -1).reshape(
        -1
    )
    own_tokens = lax.dynamic_slice_in_dim(token_req, seq_index * tile_rows, tile_rows)
    own_request = mod_req[seq_index]
    own_owner = tile_owner[seq_index]
    select = (jnp.arange(request_count, dtype=jnp.int32) == own_request).astype(jnp.float32)

    def choose_row(table):
        return jnp.dot(select, table, precision=lax.Precision.HIGHEST)

    hidden_f32 = hidden.astype(jnp.float32)
    row_mean = jnp.mean(hidden_f32, axis=1, keepdims=True)
    row_var = jnp.mean(jnp.square(hidden_f32 - row_mean), axis=1, keepdims=True)
    normed = (hidden_f32 - row_mean) * lax.rsqrt(row_var + EPSILON)
    modulated = (
        (1.0 + choose_row(mod_scale))[None, :] * normed + choose_row(mod_shift)[None, :]
    ).astype(jnp.bfloat16)
    local_width = key_cache.shape[1]
    group = group_size(seq_count, local_width // HD)
    if group > 1:
        reduced = grouped_branch(
            group, modulated, listed[0], key_cache, value_cache, text_keys, text_values,
            query_weight, key_weight, value_weight, out_weight, query_gain, key_gain,
            token_req, mod_req,
        )
    else:
        reduced = plain_branch(
            modulated, listed[0], key_cache, value_cache, text_keys, text_values,
            query_weight, key_weight, value_weight, out_weight, query_gain, key_gain,
            token_req, own_tokens, own_request,
        )
    col_count = reduced.shape[1]
    hidden_cols = lax.dynamic_slice_in_dim(hidden_f32, tp_index * col_count, col_count, 1)
    gate_cols = lax.dynamic_slice_in_dim(choose_row(mod_gate), tp_index * col_count, col_count)
    hidden_next = (hidden_cols + gate_cols[None, :] * reduced).astype(jnp.bfloat16)
    velocity = lax.psum(
        jnp.dot(hidden_next, final_weight, preferred_element_type=jnp.float32).astype(jnp.bfloat16),
        "tp",
    ).astype(jnp.float32)
    step_delta = sigma_of(step_index + 1) - sigma_of(step_index)
    own_delta = jnp.sum(select * step_delta)
    latent_next = latent + own_delta * velocity
    token_live = own_tokens >= 0
    dec_input = jnp.where(token_live[:, None], latent_next, 0.0).astype(jnp.bfloat16)
    padded = with_halo(dec_input, (("seq", 0),), IMG_W)
    prev_owner = tile_owner[jnp.maximum(seq_index - 1, 0)]
    next_owner = tile_owner[jnp.minimum(seq_index + 1, seq_count - 1)]
    same_prev = (seq_index > 0) & (prev_owner == own_owner)
    same_next = (seq_index < seq_count - 1) & (next_owner == own_owner)
    upper = jnp.where(same_prev, padded[:IMG_W], 0.0)
    lower = jnp.where(same_next, padded[IMG_W + tile_rows :], 0.0)
    framed_tokens = jnp.concatenate([upper, padded[IMG_W : IMG_W + tile_rows], lower], axis=0)
    token_rows = tile_rows // IMG_W
    pixel_ch = LAT_CH // 4
    pixels = framed_tokens.reshape(token_rows + 2, IMG_W, pixel_ch, 2, 2)
    pixels = jnp.transpose(pixels, (0, 3, 1, 4, 2)).reshape(
        2 * (token_rows + 2), 2 * IMG_W, pixel_ch
    )
    framed = pixels[1 : 2 * token_rows + 3]
    framed = jnp.pad(framed, ((0, 0), (1, 1), (0, 0)))
    patches = jnp.concatenate(
        [
            framed[row_shift : row_shift + 2 * token_rows, col_shift : col_shift + 2 * IMG_W, :]
            for row_shift in range(3)
            for col_shift in range(3)
        ],
        axis=-1,
    )
    convolved = jnp.dot(
        patches.reshape(-1, 9 * pixel_ch), conv_weight, preferred_element_type=jnp.float32
    )
    pixel_live = jnp.broadcast_to(
        token_live.reshape(token_rows, 1, IMG_W, 1), (token_rows, 2, IMG_W, 2)
    ).reshape(-1)
    decoded = jnp.where(pixel_live[:, None], convolved, 0.0).astype(jnp.bfloat16)
    return (hidden_next, latent_next, decoded)


def solution(mesh):
    return jax.shard_map(
        shards,
        mesh=mesh,
        in_specs=(
            P("seq", None),
            P("seq", None),
            P("seq", "tp"),
            P("seq", "tp"),
            P(None, None, "tp"),
            P(None, None, "tp"),
            P("seq", "tp"),
            P("seq", "tp"),
            P("seq", "tp"),
            P("seq", "tp"),
            P(),
            P(),
            P(),
            P(),
            P(),
            P("tp", None),
            P(None, "tp"),
            P(),
            P(),
            P("seq", None),
            P(),
        ),
        out_specs=(P("seq", "tp"), P("seq", None), P("seq", "tp")),
        check_vma=False,
    )
```

```python
import math

import jax
import jax.numpy as jnp
from jax import lax
from jax.experimental import pallas as pl
from jax.experimental.pallas import tpu as pltpu
from jax.sharding import PartitionSpec as P

HD = 128
LAT_CH = 64
IMG_W = 64
STEPS = 8


EPSILON = 1e-06
SIGMA_SHIFT = 3.0


def with_halo(shard, sides, width):
    for axis, dim in sides:
        devices, length = (lax.axis_size(axis), shard.shape[dim])
        up = [(i, (i + 1) % devices) for i in range(devices - 1)]
        down = [(j, i) for i, j in up]
        last = lax.slice_in_dim(shard, length - width, length, axis=dim)
        first = lax.slice_in_dim(shard, 0, width, axis=dim)
        before = lax.ppermute(last, axis, up)
        after = lax.ppermute(first, axis, down)
        shard = jnp.concatenate([before, shard, after], axis=dim)
    return shard


def tile_layout(tile_owner, image_rows, tile_rows, row_width):
    request_count = image_rows.shape[0]
    tile_count = tile_owner.shape[0]
    earlier = jnp.sum((tile_owner[None, :] < tile_owner[:, None]).astype(jnp.int32), axis=1)
    ordinal = jnp.arange(tile_count, dtype=jnp.int32) - earlier
    mod_req = jnp.minimum(tile_owner, request_count - 1)
    picked = jnp.sum(
        jnp.where(
            mod_req[:, None] == jnp.arange(request_count, dtype=jnp.int32)[None, :],
            image_rows[None, :],
            0,
        ),
        axis=1,
    )
    live_rows = jnp.where(
        tile_owner < request_count,
        jnp.clip(picked * row_width - ordinal * tile_rows, 0, tile_rows),
        0,
    )
    return (mod_req, live_rows)


def sigma_of(step_index):
    fraction = 1.0 - step_index.astype(jnp.float32) / STEPS
    return SIGMA_SHIFT * fraction / (1.0 + (SIGMA_SHIFT - 1.0) * fraction)


def head_norm(projected, head_gain):
    row_count = projected.shape[0]
    shaped = projected.reshape(row_count, -1, HD)
    inverse = lax.rsqrt(jnp.mean(jnp.square(shaped), axis=2, keepdims=True) + EPSILON)
    return shaped * inverse * head_gain


def plain_branch(
    modulated, listed_rows, key_cache, value_cache, text_keys, text_values,
    query_weight, key_weight, value_weight, out_weight, query_gain, key_gain,
    token_req, own_tokens, own_request,
):
    tile_rows = modulated.shape[0]
    listed_x = modulated[listed_rows]
    local_width = key_cache.shape[1]
    local_heads = local_width // HD
    gathered_q, gathered_k, gathered_v, gathered_out = (
        lax.all_gather(query_weight, "seq", axis=0, tiled=True),
        lax.all_gather(key_weight, "seq", axis=0, tiled=True),
        lax.all_gather(value_weight, "seq", axis=0, tiled=True),
        lax.all_gather(out_weight, "seq", axis=0, tiled=True),
    )
    query_raw = jnp.dot(modulated, gathered_q, preferred_element_type=jnp.float32)
    key_raw = jnp.dot(listed_x, gathered_k, preferred_element_type=jnp.float32)
    value_raw = jnp.dot(listed_x, gathered_v, preferred_element_type=jnp.float32)
    queries = head_norm(query_raw, query_gain).astype(jnp.bfloat16)
    fresh_keys = head_norm(key_raw, key_gain).astype(jnp.bfloat16).reshape(-1, local_width)
    fresh_values = value_raw.astype(jnp.bfloat16)
    local_keys = key_cache.at[listed_rows].set(fresh_keys)
    local_values = value_cache.at[listed_rows].set(fresh_values)
    score_scale = 1.0 / math.sqrt(HD)
    text_key_tile = lax.dynamic_index_in_dim(text_keys, own_request, 0, keepdims=False).reshape(
        -1, local_heads, HD
    )
    text_value_tile = lax.dynamic_index_in_dim(text_values, own_request, 0, keepdims=False).reshape(
        -1, local_heads, HD
    )
    text_scores = (
        jnp.einsum("qhd,khd->hqk", queries, text_key_tile, preferred_element_type=jnp.float32)
        * score_scale
    )
    row_max = jnp.max(text_scores, axis=2)
    text_exp = jnp.exp(text_scores - row_max[..., None])
    row_sum = jnp.sum(text_exp, axis=2)
    weighted = jnp.einsum(
        "hqk,khd->hqd",
        text_exp.astype(jnp.bfloat16),
        text_value_tile,
        preferred_element_type=jnp.float32,
    )

    def attend(state_now, key_tile, value_tile, key_owner):
        old_max, old_sum, old_weighted = state_now
        allowed = (key_owner[None, :] == own_tokens[:, None]) & (own_tokens[:, None] >= 0)
        key_heads = key_tile.reshape(-1, local_heads, HD)
        value_heads = value_tile.reshape(-1, local_heads, HD)
        scores = (
            jnp.einsum("qhd,khd->hqk", queries, key_heads, preferred_element_type=jnp.float32)
            * score_scale
        )
        scores = jnp.where(allowed[None], scores, -jnp.inf)
        new_max = jnp.maximum(old_max, jnp.max(scores, axis=2))
        shrink = jnp.exp(old_max - new_max)
        exp_scores = jnp.exp(scores - new_max[..., None])
        new_sum = old_sum * shrink + jnp.sum(exp_scores, axis=2)
        new_weighted = old_weighted * shrink[..., None] + jnp.einsum(
            "hqk,khd->hqd",
            exp_scores.astype(jnp.bfloat16),
            value_heads,
            preferred_element_type=jnp.float32,
        )
        return (new_max, new_sum, new_weighted)

    pieces = (
        lax.all_gather(local_keys, "seq", axis=0, tiled=True),
        lax.all_gather(local_values, "seq", axis=0, tiled=True),
    )
    length = pieces[0].shape[0]
    key_owner = token_req
    key_block = 1024
    block_count = length // key_block
    stacked = (
        pieces[0].reshape(block_count, key_block, -1),
        pieces[1].reshape(block_count, key_block, -1),
        key_owner.reshape(block_count, key_block),
    )

    def scan_step(state_mid, blocks):
        return (attend(state_mid, blocks[0], blocks[1], blocks[2]), None)

    row_max, row_sum, weighted = lax.scan(scan_step, (row_max, row_sum, weighted), stacked)[0]
    attended = (
        jnp.transpose(weighted / row_sum[..., None], (1, 0, 2))
        .reshape(tile_rows, local_width)
        .astype(jnp.bfloat16)
    )
    partial_out = lax.dot_general(
        attended, gathered_out, (((1,), (1,)), ((), ())), preferred_element_type=jnp.float32
    )
    reduced = lax.psum_scatter(
        partial_out.astype(jnp.bfloat16), "tp", scatter_dimension=1, tiled=True
    ).astype(jnp.float32)
    return reduced


GROUP = 4


def group_size(seq_count, local_heads):
    if seq_count == GROUP * GROUP and seq_count == 2 * local_heads:
        return GROUP
    return 1


def attention_kernel(
    request_ref, place_ref, q_ref, k_ref, v_ref, tk_ref, tv_ref, key_req_ref, tok_req_ref, o_ref
):
    scale = 1.0 / math.sqrt(HD)
    q = q_ref[...]
    dims = (((1,), (1,)), ((), ()))
    s_text = lax.dot_general(q, tk_ref[0], dims, preferred_element_type=jnp.float32) * scale
    s_img = lax.dot_general(q, k_ref[...], dims, preferred_element_type=jnp.float32) * scale
    own = tok_req_ref[...]
    allowed = (key_req_ref[...] == own) & (own >= 0)
    s_img = jnp.where(allowed, s_img, -jnp.inf)
    top = jnp.maximum(
        jnp.max(s_text, axis=1, keepdims=True), jnp.max(s_img, axis=1, keepdims=True)
    )
    e_text = jnp.exp(s_text - top)
    e_img = jnp.exp(s_img - top)
    total = jnp.sum(e_text, axis=1, keepdims=True) + jnp.sum(e_img, axis=1, keepdims=True)
    acc = jnp.dot(e_text.astype(jnp.bfloat16), tv_ref[0], preferred_element_type=jnp.float32)
    acc += jnp.dot(e_img.astype(jnp.bfloat16), v_ref[...], preferred_element_type=jnp.float32)
    o_ref[...] = (acc / total).astype(jnp.bfloat16)


def attention(queries, keys, values, text_keys, text_values, requests, place, token_req, own_req):
    rows, width = queries.shape
    length = keys.shape[0]
    text = text_keys.shape[1]
    heads = width // HD
    tiles = requests.shape[0]
    tile_rows = rows // tiles
    grid_spec = pltpu.PrefetchScalarGridSpec(
        num_scalar_prefetch=2,
        grid=(heads, tiles),
        in_specs=[
            pl.BlockSpec((tile_rows, HD), lambda h, t, req, pos: (t, h)),
            pl.BlockSpec((length, HD), lambda h, t, req, pos: (0, h)),
            pl.BlockSpec((length, HD), lambda h, t, req, pos: (0, h)),
            pl.BlockSpec((1, text, HD), lambda h, t, req, pos: (req[t], 0, pos[0] * heads + h)),
            pl.BlockSpec((1, text, HD), lambda h, t, req, pos: (req[t], 0, pos[0] * heads + h)),
            pl.BlockSpec((1, length), lambda h, t, req, pos: (0, 0)),
            pl.BlockSpec((tile_rows, 1), lambda h, t, req, pos: (t, 0)),
        ],
        out_specs=pl.BlockSpec((tile_rows, HD), lambda h, t, req, pos: (t, h)),
    )
    return pl.pallas_call(
        attention_kernel,
        grid_spec=grid_spec,
        out_shape=jax.ShapeDtypeStruct((rows, width), jnp.bfloat16),
        compiler_params=pltpu.CompilerParams(vmem_limit_bytes=32 * 1024 * 1024),
        cost_estimate=pl.CostEstimate(
            flops=4 * rows * width * (length + text),
            bytes_accessed=8 * length * width,
            transcendentals=rows * heads * (length + text),
        ),
    )(
        requests, place, queries, keys, values, text_keys, text_values,
        token_req.reshape(1, -1), own_req.reshape(-1, 1),
    )


def interleave(first, second):
    rows = first.shape[0]
    both = jnp.stack([first.reshape(rows, -1, HD), second.reshape(rows, -1, HD)], axis=2)
    return both.reshape(rows, -1)


def grouped_branch(
    group, modulated, listed_rows, key_cache, value_cache, text_keys, text_values,
    query_weight, key_weight, value_weight, out_weight, query_gain, key_gain,
    token_req, mod_req,
):
    tile_rows, model = modulated.shape
    seq_count = lax.axis_size("seq")
    tp_count = lax.axis_size("tp")
    seq_index = lax.axis_index("seq")
    tp_index = lax.axis_index("tp")
    lines = seq_count // group
    place = lax.rem(seq_index, group)
    line = seq_index // group
    core = lax.rem(seq_index, 2)
    side = place // 2
    width = key_cache.shape[1] // group
    depth = query_weight.shape[0]
    half_rows = group * tile_rows // 2
    inner = [[z * group + p for p in range(group)] for z in range(lines)]
    outer = [[z * group + p for z in range(lines)] for p in range(group)]
    turns = [
        [(z * group + p, p * group + (z + k) % group) for z in range(lines) for p in range(group)]
        for k in range(group)
    ]

    def line_gather(block):
        return lax.all_gather(block, "seq", axis=0, axis_index_groups=outer, tiled=True)

    moved = jnp.concatenate(
        [interleave(key_weight, value_weight), interleave(key_cache, value_cache)], axis=0
    )
    moved = lax.all_to_all(moved, "seq", split_axis=1, concat_axis=0, tiled=True)
    moved = moved.reshape(seq_count, -1, HD)
    head_weight = moved[:, :depth].reshape(-1, HD)
    head_cache = moved[:, depth:]

    listed_x = jnp.concatenate(
        [
            modulated[listed_rows],
            jnp.broadcast_to(listed_rows[:, None], (listed_rows.shape[0], HD)).astype(
                jnp.bfloat16
            ),
        ],
        axis=1,
    )
    all_listed = lax.all_gather(listed_x, "seq", axis=0, tiled=True)
    tokens = modulated
    query_w = line_gather(
        lax.all_to_all(
            query_weight, "seq", split_axis=1, concat_axis=0, axis_index_groups=inner, tiled=True
        )
    )
    tokens = lax.all_gather(modulated, "seq", axis=0, axis_index_groups=inner, tiled=True)
    fresh_raw = jnp.dot(all_listed[:, :model], head_weight, preferred_element_type=jnp.float32)
    fresh_keys = head_norm(fresh_raw, key_gain).reshape(-1, HD)
    fresh = jnp.where(core == 0, fresh_keys, fresh_raw).astype(jnp.bfloat16)
    fresh = fresh.reshape(seq_count, -1, HD)
    spots = all_listed[:, model].astype(jnp.int32).reshape(seq_count, 1, -1)
    onehot = spots == jnp.arange(tile_rows, dtype=jnp.int32)[None, :, None]
    placed = jnp.einsum(
        "trl,tld->trd", onehot.astype(jnp.bfloat16), fresh, preferred_element_type=jnp.float32
    ).astype(jnp.bfloat16)
    mine = jnp.where(jnp.any(onehot, axis=2, keepdims=True), placed, head_cache)
    mine = mine.reshape(-1, HD)
    other = lax.ppermute(mine, "seq", [(i, i ^ 1) for i in range(seq_count)])
    keys = jnp.where(core == 0, mine, other)
    values = jnp.where(core == 0, other, mine)

    query_raw = jnp.dot(tokens, query_w, preferred_element_type=jnp.float32)
    queries = head_norm(query_raw, query_gain).astype(jnp.bfloat16).reshape(-1, width)
    got_queries, got_requests, got_tokens = [], [], []
    for k in range(group):
        target = lax.rem(line + k, group)
        block = lax.dynamic_slice(
            queries, (lax.rem(target, 2) * half_rows, (target // 2) * HD), (half_rows, HD)
        )
        got_queries.append(lax.ppermute(block, "seq", turns[k]))
        tile = lax.rem(place + group - k, group) * group + core * (group // 2)
        got_requests.append(lax.dynamic_slice_in_dim(mod_req, tile, group // 2))
        got_tokens.append(lax.dynamic_slice_in_dim(token_req, tile * tile_rows, half_rows))
    out_w = line_gather(out_weight)
    attended = attention(
        jnp.concatenate(got_queries, axis=0), keys, values, text_keys, text_values,
        jnp.concatenate(got_requests), (seq_index // 2).reshape(1),
        token_req, jnp.concatenate(got_tokens),
    )
    own_heads = jnp.zeros((2 * half_rows, width), jnp.bfloat16)
    for k in range(group):
        block = attended[k * half_rows : (k + 1) * half_rows]
        back = lax.ppermute(block, "seq", [(j, i) for i, j in turns[k]])
        origin = lax.rem(line + k, group)
        own_heads = lax.dynamic_update_slice(
            own_heads, back, (lax.rem(origin, 2) * half_rows, (origin // 2) * HD)
        )
    all_heads = jnp.zeros((2 * half_rows, group * width), jnp.bfloat16)
    for k in range(group):
        got = own_heads
        if k > 0:
            got = lax.ppermute(own_heads, "seq", [(i, i ^ k) for i in range(seq_count)])
        all_heads = lax.dynamic_update_slice(
            all_heads, got, (jnp.int32(0), jnp.bitwise_xor(place, k) * width)
        )
    partial_out = lax.dot_general(
        all_heads, out_w, (((1,), (1,)), ((), ())), preferred_element_type=jnp.float32
    ).astype(jnp.bfloat16)
    share = partial_out.shape[1] // tp_count
    pieces = jnp.zeros((group, tile_rows, share), jnp.float32)
    for k in range(group):
        peer = jnp.bitwise_xor(place, k)
        total = 0.0
        for j in range(tp_count):
            block = lax.dynamic_slice(
                partial_out,
                (peer * tile_rows, lax.rem(tp_index + j, tp_count) * share),
                (tile_rows, share),
            )
            if k > 0 or j > 0:
                block = lax.ppermute(
                    block,
                    ("seq", "tp"),
                    [
                        (i * tp_count + t, (i ^ k) * tp_count + (t + j) % tp_count)
                        for i in range(seq_count)
                        for t in range(tp_count)
                    ],
                )
            total = total + block.astype(jnp.float32)
        pieces = lax.dynamic_update_slice(pieces, total[None], (peer, jnp.int32(0), jnp.int32(0)))
    pieces = pieces.reshape(group, tile_rows, -1, depth)
    return jnp.transpose(pieces, (1, 2, 0, 3)).reshape(tile_rows, -1)


def shards(
    hidden,
    latent,
    key_cache,
    value_cache,
    text_keys,
    text_values,
    query_weight,
    key_weight,
    value_weight,
    out_weight,
    query_gain,
    key_gain,
    mod_shift,
    mod_scale,
    mod_gate,
    final_weight,
    conv_weight,
    image_rows,
    tile_owner,
    listed,
    step_index,
):
    tile_rows = hidden.shape[0]
    seq_count = lax.axis_size("seq")
    seq_index = lax.axis_index("seq")
    tp_index = lax.axis_index("tp")
    request_count = image_rows.shape[0]
    mod_req, live_rows = tile_layout(tile_owner, image_rows, tile_rows, IMG_W)
    row_index = jnp.arange(tile_rows, dtype=jnp.int32)
    token_req = jnp.where(row_index[None, :] < live_rows[:, None], tile_owner[:, None], -1).reshape(
        -1
    )
    own_tokens = lax.dynamic_slice_in_dim(token_req, seq_index * tile_rows, tile_rows)
    own_request = mod_req[seq_index]
    own_owner = tile_owner[seq_index]
    select = (jnp.arange(request_count, dtype=jnp.int32) == own_request).astype(jnp.float32)

    def choose_row(table):
        return jnp.dot(select, table, precision=lax.Precision.HIGHEST)

    hidden_f32 = hidden.astype(jnp.float32)
    row_mean = jnp.mean(hidden_f32, axis=1, keepdims=True)
    row_var = jnp.mean(jnp.square(hidden_f32 - row_mean), axis=1, keepdims=True)
    normed = (hidden_f32 - row_mean) * lax.rsqrt(row_var + EPSILON)
    modulated = (
        (1.0 + choose_row(mod_scale))[None, :] * normed + choose_row(mod_shift)[None, :]
    ).astype(jnp.bfloat16)
    local_width = key_cache.shape[1]
    group = group_size(seq_count, local_width // HD)
    if group > 1:
        reduced = grouped_branch(
            group, modulated, listed[0], key_cache, value_cache, text_keys, text_values,
            query_weight, key_weight, value_weight, out_weight, query_gain, key_gain,
            token_req, mod_req,
        )
    else:
        reduced = plain_branch(
            modulated, listed[0], key_cache, value_cache, text_keys, text_values,
            query_weight, key_weight, value_weight, out_weight, query_gain, key_gain,
            token_req, own_tokens, own_request,
        )
    col_count = reduced.shape[1]
    hidden_cols = lax.dynamic_slice_in_dim(hidden_f32, tp_index * col_count, col_count, 1)
    gate_cols = lax.dynamic_slice_in_dim(choose_row(mod_gate), tp_index * col_count, col_count)
    hidden_next = (hidden_cols + gate_cols[None, :] * reduced).astype(jnp.bfloat16)
    velocity = jnp.dot(hidden_next, final_weight, preferred_element_type=jnp.float32).astype(
        jnp.bfloat16
    )
    if lax.axis_size("tp") == 2:
        velocity = velocity.astype(jnp.float32) + lax.ppermute(
            velocity, "tp", [(0, 1), (1, 0)]
        ).astype(jnp.float32)
    else:
        velocity = lax.psum(velocity, "tp").astype(jnp.float32)
    step_delta = sigma_of(step_index + 1) - sigma_of(step_index)
    own_delta = jnp.sum(select * step_delta)
    latent_next = latent + own_delta * velocity
    token_live = own_tokens >= 0
    dec_input = jnp.where(token_live[:, None], latent_next, 0.0).astype(jnp.bfloat16)
    padded = with_halo(dec_input, (("seq", 0),), IMG_W)
    prev_owner = tile_owner[jnp.maximum(seq_index - 1, 0)]
    next_owner = tile_owner[jnp.minimum(seq_index + 1, seq_count - 1)]
    same_prev = (seq_index > 0) & (prev_owner == own_owner)
    same_next = (seq_index < seq_count - 1) & (next_owner == own_owner)
    upper = jnp.where(same_prev, padded[:IMG_W], 0.0)
    lower = jnp.where(same_next, padded[IMG_W + tile_rows :], 0.0)
    framed_tokens = jnp.concatenate([upper, padded[IMG_W : IMG_W + tile_rows], lower], axis=0)
    token_rows = tile_rows // IMG_W
    pixel_ch = LAT_CH // 4
    pixels = framed_tokens.reshape(token_rows + 2, IMG_W, pixel_ch, 2, 2)
    pixels = jnp.transpose(pixels, (0, 3, 1, 4, 2)).reshape(
        2 * (token_rows + 2), 2 * IMG_W, pixel_ch
    )
    framed = pixels[1 : 2 * token_rows + 3]
    framed = jnp.pad(framed, ((0, 0), (1, 1), (0, 0)))
    patches = jnp.concatenate(
        [
            framed[row_shift : row_shift + 2 * token_rows, col_shift : col_shift + 2 * IMG_W, :]
            for row_shift in range(3)
            for col_shift in range(3)
        ],
        axis=-1,
    )
    convolved = jnp.dot(
        patches.reshape(-1, 9 * pixel_ch), conv_weight, preferred_element_type=jnp.float32
    )
    pixel_live = jnp.broadcast_to(
        token_live.reshape(token_rows, 1, IMG_W, 1), (token_rows, 2, IMG_W, 2)
    ).reshape(-1)
    decoded = jnp.where(pixel_live[:, None], convolved, 0.0).astype(jnp.bfloat16)
    return (hidden_next, latent_next, decoded)


def solution(mesh):
    return jax.shard_map(
        shards,
        mesh=mesh,
        in_specs=(
            P("seq", None),
            P("seq", None),
            P("seq", "tp"),
            P("seq", "tp"),
            P(None, None, "tp"),
            P(None, None, "tp"),
            P("seq", "tp"),
            P("seq", "tp"),
            P("seq", "tp"),
            P("seq", "tp"),
            P(),
            P(),
            P(),
            P(),
            P(),
            P("tp", None),
            P(None, "tp"),
            P(),
            P(),
            P("seq", None),
            P(),
        ),
        out_specs=(P("seq", "tp"), P("seq", None), P("seq", "tp")),
        check_vma=False,
    )
```

```python
import math

import jax
import jax.numpy as jnp
from jax import lax
from jax.experimental import pallas as pl
from jax.experimental.pallas import tpu as pltpu
from jax.sharding import PartitionSpec as P

HD = 128
LAT_CH = 64
IMG_W = 64
STEPS = 8


EPSILON = 1e-06
SIGMA_SHIFT = 3.0


def with_halo(shard, sides, width):
    for axis, dim in sides:
        devices, length = (lax.axis_size(axis), shard.shape[dim])
        up = [(i, (i + 1) % devices) for i in range(devices - 1)]
        down = [(j, i) for i, j in up]
        last = lax.slice_in_dim(shard, length - width, length, axis=dim)
        first = lax.slice_in_dim(shard, 0, width, axis=dim)
        before = lax.ppermute(last, axis, up)
        after = lax.ppermute(first, axis, down)
        shard = jnp.concatenate([before, shard, after], axis=dim)
    return shard


def tile_layout(tile_owner, image_rows, tile_rows, row_width):
    request_count = image_rows.shape[0]
    tile_count = tile_owner.shape[0]
    earlier = jnp.sum((tile_owner[None, :] < tile_owner[:, None]).astype(jnp.int32), axis=1)
    ordinal = jnp.arange(tile_count, dtype=jnp.int32) - earlier
    mod_req = jnp.minimum(tile_owner, request_count - 1)
    picked = jnp.sum(
        jnp.where(
            mod_req[:, None] == jnp.arange(request_count, dtype=jnp.int32)[None, :],
            image_rows[None, :],
            0,
        ),
        axis=1,
    )
    live_rows = jnp.where(
        tile_owner < request_count,
        jnp.clip(picked * row_width - ordinal * tile_rows, 0, tile_rows),
        0,
    )
    return (mod_req, live_rows)


def sigma_of(step_index):
    fraction = 1.0 - step_index.astype(jnp.float32) / STEPS
    return SIGMA_SHIFT * fraction / (1.0 + (SIGMA_SHIFT - 1.0) * fraction)


def head_norm(projected, head_gain):
    row_count = projected.shape[0]
    shaped = projected.reshape(row_count, -1, HD)
    inverse = lax.rsqrt(jnp.mean(jnp.square(shaped), axis=2, keepdims=True) + EPSILON)
    return shaped * inverse * head_gain


def plain_branch(
    modulated, listed_rows, key_cache, value_cache, text_keys, text_values,
    query_weight, key_weight, value_weight, out_weight, query_gain, key_gain,
    token_req, own_tokens, own_request,
):
    tile_rows = modulated.shape[0]
    listed_x = modulated[listed_rows]
    local_width = key_cache.shape[1]
    local_heads = local_width // HD
    gathered_q, gathered_k, gathered_v, gathered_out = (
        lax.all_gather(query_weight, "seq", axis=0, tiled=True),
        lax.all_gather(key_weight, "seq", axis=0, tiled=True),
        lax.all_gather(value_weight, "seq", axis=0, tiled=True),
        lax.all_gather(out_weight, "seq", axis=0, tiled=True),
    )
    query_raw = jnp.dot(modulated, gathered_q, preferred_element_type=jnp.float32)
    key_raw = jnp.dot(listed_x, gathered_k, preferred_element_type=jnp.float32)
    value_raw = jnp.dot(listed_x, gathered_v, preferred_element_type=jnp.float32)
    queries = head_norm(query_raw, query_gain).astype(jnp.bfloat16)
    fresh_keys = head_norm(key_raw, key_gain).astype(jnp.bfloat16).reshape(-1, local_width)
    fresh_values = value_raw.astype(jnp.bfloat16)
    local_keys = key_cache.at[listed_rows].set(fresh_keys)
    local_values = value_cache.at[listed_rows].set(fresh_values)
    score_scale = 1.0 / math.sqrt(HD)
    text_key_tile = lax.dynamic_index_in_dim(text_keys, own_request, 0, keepdims=False).reshape(
        -1, local_heads, HD
    )
    text_value_tile = lax.dynamic_index_in_dim(text_values, own_request, 0, keepdims=False).reshape(
        -1, local_heads, HD
    )
    text_scores = (
        jnp.einsum("qhd,khd->hqk", queries, text_key_tile, preferred_element_type=jnp.float32)
        * score_scale
    )
    row_max = jnp.max(text_scores, axis=2)
    text_exp = jnp.exp(text_scores - row_max[..., None])
    row_sum = jnp.sum(text_exp, axis=2)
    weighted = jnp.einsum(
        "hqk,khd->hqd",
        text_exp.astype(jnp.bfloat16),
        text_value_tile,
        preferred_element_type=jnp.float32,
    )

    def attend(state_now, key_tile, value_tile, key_owner):
        old_max, old_sum, old_weighted = state_now
        allowed = (key_owner[None, :] == own_tokens[:, None]) & (own_tokens[:, None] >= 0)
        key_heads = key_tile.reshape(-1, local_heads, HD)
        value_heads = value_tile.reshape(-1, local_heads, HD)
        scores = (
            jnp.einsum("qhd,khd->hqk", queries, key_heads, preferred_element_type=jnp.float32)
            * score_scale
        )
        scores = jnp.where(allowed[None], scores, -jnp.inf)
        new_max = jnp.maximum(old_max, jnp.max(scores, axis=2))
        shrink = jnp.exp(old_max - new_max)
        exp_scores = jnp.exp(scores - new_max[..., None])
        new_sum = old_sum * shrink + jnp.sum(exp_scores, axis=2)
        new_weighted = old_weighted * shrink[..., None] + jnp.einsum(
            "hqk,khd->hqd",
            exp_scores.astype(jnp.bfloat16),
            value_heads,
            preferred_element_type=jnp.float32,
        )
        return (new_max, new_sum, new_weighted)

    pieces = (
        lax.all_gather(local_keys, "seq", axis=0, tiled=True),
        lax.all_gather(local_values, "seq", axis=0, tiled=True),
    )
    length = pieces[0].shape[0]
    key_owner = token_req
    key_block = 1024
    block_count = length // key_block
    stacked = (
        pieces[0].reshape(block_count, key_block, -1),
        pieces[1].reshape(block_count, key_block, -1),
        key_owner.reshape(block_count, key_block),
    )

    def scan_step(state_mid, blocks):
        return (attend(state_mid, blocks[0], blocks[1], blocks[2]), None)

    row_max, row_sum, weighted = lax.scan(scan_step, (row_max, row_sum, weighted), stacked)[0]
    attended = (
        jnp.transpose(weighted / row_sum[..., None], (1, 0, 2))
        .reshape(tile_rows, local_width)
        .astype(jnp.bfloat16)
    )
    partial_out = lax.dot_general(
        attended, gathered_out, (((1,), (1,)), ((), ())), preferred_element_type=jnp.float32
    )
    reduced = lax.psum_scatter(
        partial_out.astype(jnp.bfloat16), "tp", scatter_dimension=1, tiled=True
    ).astype(jnp.float32)
    return reduced


GROUP = 4


def group_size(seq_count, local_heads):
    if seq_count == GROUP * GROUP and seq_count == 2 * local_heads:
        return GROUP
    return 1


def attention_kernel(
    request_ref, place_ref, q_ref, k_ref, v_ref, tk_ref, tv_ref, key_req_ref, tok_req_ref, o_ref
):
    scale = 1.0 / math.sqrt(HD)
    q = q_ref[...]
    dims = (((1,), (1,)), ((), ()))
    s_text = lax.dot_general(q, tk_ref[0], dims, preferred_element_type=jnp.float32) * scale
    s_img = lax.dot_general(q, k_ref[...], dims, preferred_element_type=jnp.float32) * scale
    own = tok_req_ref[...]
    allowed = (key_req_ref[...] == own) & (own >= 0)
    s_img = jnp.where(allowed, s_img, -jnp.inf)
    top = jnp.maximum(
        jnp.max(s_text, axis=1, keepdims=True), jnp.max(s_img, axis=1, keepdims=True)
    )
    e_text = jnp.exp(s_text - top)
    e_img = jnp.exp(s_img - top)
    total = jnp.sum(e_text, axis=1, keepdims=True) + jnp.sum(e_img, axis=1, keepdims=True)
    acc = jnp.dot(e_text.astype(jnp.bfloat16), tv_ref[0], preferred_element_type=jnp.float32)
    acc += jnp.dot(e_img.astype(jnp.bfloat16), v_ref[...], preferred_element_type=jnp.float32)
    o_ref[...] = (acc / total).astype(jnp.bfloat16)


def attention(queries, keys, values, text_keys, text_values, requests, place, token_req, own_req):
    rows, width = queries.shape
    length = keys.shape[0]
    text = text_keys.shape[1]
    heads = width // HD
    tiles = requests.shape[0]
    tile_rows = rows // tiles
    grid_spec = pltpu.PrefetchScalarGridSpec(
        num_scalar_prefetch=2,
        grid=(heads, tiles),
        in_specs=[
            pl.BlockSpec((tile_rows, HD), lambda h, t, req, pos: (t, h)),
            pl.BlockSpec((length, HD), lambda h, t, req, pos: (0, h)),
            pl.BlockSpec((length, HD), lambda h, t, req, pos: (0, h)),
            pl.BlockSpec((1, text, HD), lambda h, t, req, pos: (req[t], 0, pos[0] * heads + h)),
            pl.BlockSpec((1, text, HD), lambda h, t, req, pos: (req[t], 0, pos[0] * heads + h)),
            pl.BlockSpec((1, length), lambda h, t, req, pos: (0, 0)),
            pl.BlockSpec((tile_rows, 1), lambda h, t, req, pos: (t, 0)),
        ],
        out_specs=pl.BlockSpec((tile_rows, HD), lambda h, t, req, pos: (t, h)),
    )
    return pl.pallas_call(
        attention_kernel,
        grid_spec=grid_spec,
        out_shape=jax.ShapeDtypeStruct((rows, width), jnp.bfloat16),
        compiler_params=pltpu.CompilerParams(vmem_limit_bytes=32 * 1024 * 1024),
        cost_estimate=pl.CostEstimate(
            flops=4 * rows * width * (length + text),
            bytes_accessed=8 * length * width,
            transcendentals=rows * heads * (length + text),
        ),
    )(
        requests, place, queries, keys, values, text_keys, text_values,
        token_req.reshape(1, -1), own_req.reshape(-1, 1),
    )


def interleave(first, second):
    rows = first.shape[0]
    both = jnp.stack([first.reshape(rows, -1, HD), second.reshape(rows, -1, HD)], axis=2)
    return both.reshape(rows, -1)


def grouped_branch(
    group, modulated, listed_rows, key_cache, value_cache, text_keys, text_values,
    query_weight, key_weight, value_weight, out_weight, query_gain, key_gain,
    token_req, mod_req,
):
    tile_rows, model = modulated.shape
    seq_count = lax.axis_size("seq")
    tp_count = lax.axis_size("tp")
    seq_index = lax.axis_index("seq")
    tp_index = lax.axis_index("tp")
    lines = seq_count // group
    place = lax.rem(seq_index, group)
    line = seq_index // group
    core = lax.rem(seq_index, 2)
    side = place // 2
    width = key_cache.shape[1] // group
    depth = query_weight.shape[0]
    half_rows = group * tile_rows // 2
    inner = [[z * group + p for p in range(group)] for z in range(lines)]
    turns = [
        [(z * group + p, p * group + (z + k) % group) for z in range(lines) for p in range(group)]
        for k in range(group)
    ]

    def line_gather(block):
        full = jnp.zeros((lines,) + block.shape, block.dtype)
        for k in range(lines):
            got = block
            if k > 0:
                got = lax.ppermute(
                    block, "seq", [(i, (i + k * group) % seq_count) for i in range(seq_count)]
                )
            full = lax.dynamic_update_slice(
                full, got[None], (lax.rem(line + lines - k, lines), jnp.int32(0), jnp.int32(0))
            )
        return full.reshape(-1, block.shape[1])

    def paired(block, flip, position):
        got = lax.ppermute(block, "seq", [(i, i ^ flip) for i in range(seq_count)])
        first = jnp.where(position == 0, block, got)
        second = jnp.where(position == 0, got, block)
        return jnp.concatenate([first, second], axis=0)

    def plane_gather(block):
        return paired(paired(block, 2, side), 1, core)

    def spot_of(at):
        return lax.rem(at, 2) * 2 + at // 2

    def tile_order(rows):
        shaped = rows.reshape((2, 2, lines, -1) + rows.shape[1:])
        return jnp.swapaxes(shaped, 0, 2).reshape((seq_count, -1) + rows.shape[1:])

    moved = jnp.concatenate(
        [interleave(key_weight, value_weight), interleave(key_cache, value_cache)], axis=0
    )
    moved = lax.all_to_all(moved, "seq", split_axis=1, concat_axis=0, tiled=True)
    moved = moved.reshape(seq_count, -1, HD)
    head_weight = moved[:, :depth].reshape(-1, HD)
    head_cache = moved[:, depth:]

    listed_x = jnp.concatenate(
        [
            modulated[listed_rows],
            jnp.broadcast_to(listed_rows[:, None], (listed_rows.shape[0], HD)).astype(
                jnp.bfloat16
            ),
        ],
        axis=1,
    )
    all_listed = plane_gather(line_gather(listed_x))
    query_w = line_gather(
        lax.all_to_all(
            query_weight, "seq", split_axis=1, concat_axis=0, axis_index_groups=inner, tiled=True
        )
    )
    tokens = plane_gather(modulated)
    fresh_raw = jnp.dot(all_listed[:, :model], head_weight, preferred_element_type=jnp.float32)
    fresh_keys = head_norm(fresh_raw, key_gain).reshape(-1, HD)
    fresh = jnp.where(core == 0, fresh_keys, fresh_raw).astype(jnp.bfloat16)
    fresh = tile_order(fresh)
    spots = tile_order(all_listed[:, model].astype(jnp.int32))[:, None, :]
    onehot = spots == jnp.arange(tile_rows, dtype=jnp.int32)[None, :, None]
    placed = jnp.einsum(
        "trl,tld->trd", onehot.astype(jnp.bfloat16), fresh, preferred_element_type=jnp.float32
    ).astype(jnp.bfloat16)
    mine = jnp.where(jnp.any(onehot, axis=2, keepdims=True), placed, head_cache)
    mine = mine.reshape(-1, HD)
    other = lax.ppermute(mine, "seq", [(i, i ^ 1) for i in range(seq_count)])
    keys = jnp.where(core == 0, mine, other)
    values = jnp.where(core == 0, other, mine)

    query_raw = jnp.dot(tokens, query_w, preferred_element_type=jnp.float32)
    queries = head_norm(query_raw, query_gain).astype(jnp.bfloat16).reshape(-1, width)
    got_queries, got_requests, got_tokens = [], [], []
    for k in range(group):
        target = lax.rem(line + k, group)
        block = lax.dynamic_slice(
            queries, (lax.rem(target, 2) * half_rows, (target // 2) * HD), (half_rows, HD)
        )
        got_queries.append(lax.ppermute(block, "seq", turns[k]))
        for half in range(2):
            tile = lax.rem(place + group - k, group) * group + core + 2 * half
            got_requests.append(lax.dynamic_slice_in_dim(mod_req, tile, 1))
            got_tokens.append(lax.dynamic_slice_in_dim(token_req, tile * tile_rows, tile_rows))
    out_w = line_gather(lax.optimization_barrier((out_weight, moved))[0])
    attended = attention(
        jnp.concatenate(got_queries, axis=0), keys, values, text_keys, text_values,
        jnp.concatenate(got_requests), (seq_index // 2).reshape(1),
        token_req, jnp.concatenate(got_tokens),
    )
    own_heads = jnp.zeros((2 * half_rows, width), jnp.bfloat16)
    for k in range(group):
        block = attended[k * half_rows : (k + 1) * half_rows]
        back = lax.ppermute(block, "seq", [(j, i) for i, j in turns[k]])
        origin = lax.rem(line + k, group)
        own_heads = lax.dynamic_update_slice(
            own_heads, back, (lax.rem(origin, 2) * half_rows, (origin // 2) * HD)
        )
    all_heads = jnp.zeros((2 * half_rows, group * width), jnp.bfloat16)
    for k in range(group):
        got = own_heads
        if k > 0:
            got = lax.ppermute(own_heads, "seq", [(i, i ^ k) for i in range(seq_count)])
        all_heads = lax.dynamic_update_slice(
            all_heads, got, (jnp.int32(0), jnp.bitwise_xor(place, k) * width)
        )
    partial_out = lax.dot_general(
        all_heads, out_w, (((1,), (1,)), ((), ())), preferred_element_type=jnp.float32
    ).astype(jnp.bfloat16)
    share = partial_out.shape[1] // tp_count
    pieces = jnp.zeros((group, tile_rows, share), jnp.float32)
    for k in range(group):
        peer = jnp.bitwise_xor(place, k)
        total = 0.0
        for j in range(tp_count):
            block = lax.dynamic_slice(
                partial_out,
                (spot_of(peer) * tile_rows, lax.rem(tp_index + j, tp_count) * share),
                (tile_rows, share),
            )
            if k > 0 or j > 0:
                block = lax.ppermute(
                    block,
                    ("seq", "tp"),
                    [
                        (i * tp_count + t, (i ^ k) * tp_count + (t + j) % tp_count)
                        for i in range(seq_count)
                        for t in range(tp_count)
                    ],
                )
            total = total + block.astype(jnp.float32)
        pieces = lax.dynamic_update_slice(pieces, total[None], (peer, jnp.int32(0), jnp.int32(0)))
    pieces = pieces.reshape(group, tile_rows, -1, depth)
    return jnp.transpose(pieces, (1, 2, 0, 3)).reshape(tile_rows, -1)


def shards(
    hidden,
    latent,
    key_cache,
    value_cache,
    text_keys,
    text_values,
    query_weight,
    key_weight,
    value_weight,
    out_weight,
    query_gain,
    key_gain,
    mod_shift,
    mod_scale,
    mod_gate,
    final_weight,
    conv_weight,
    image_rows,
    tile_owner,
    listed,
    step_index,
):
    tile_rows = hidden.shape[0]
    seq_count = lax.axis_size("seq")
    seq_index = lax.axis_index("seq")
    tp_index = lax.axis_index("tp")
    request_count = image_rows.shape[0]
    mod_req, live_rows = tile_layout(tile_owner, image_rows, tile_rows, IMG_W)
    row_index = jnp.arange(tile_rows, dtype=jnp.int32)
    token_req = jnp.where(row_index[None, :] < live_rows[:, None], tile_owner[:, None], -1).reshape(
        -1
    )
    own_tokens = lax.dynamic_slice_in_dim(token_req, seq_index * tile_rows, tile_rows)
    own_request = mod_req[seq_index]
    own_owner = tile_owner[seq_index]
    select = (jnp.arange(request_count, dtype=jnp.int32) == own_request).astype(jnp.float32)

    def choose_row(table):
        return jnp.dot(select, table, precision=lax.Precision.HIGHEST)

    hidden_f32 = hidden.astype(jnp.float32)
    row_mean = jnp.mean(hidden_f32, axis=1, keepdims=True)
    row_var = jnp.mean(jnp.square(hidden_f32 - row_mean), axis=1, keepdims=True)
    normed = (hidden_f32 - row_mean) * lax.rsqrt(row_var + EPSILON)
    modulated = (
        (1.0 + choose_row(mod_scale))[None, :] * normed + choose_row(mod_shift)[None, :]
    ).astype(jnp.bfloat16)
    local_width = key_cache.shape[1]
    group = group_size(seq_count, local_width // HD)
    if group > 1:
        reduced = grouped_branch(
            group, modulated, listed[0], key_cache, value_cache, text_keys, text_values,
            query_weight, key_weight, value_weight, out_weight, query_gain, key_gain,
            token_req, mod_req,
        )
    else:
        reduced = plain_branch(
            modulated, listed[0], key_cache, value_cache, text_keys, text_values,
            query_weight, key_weight, value_weight, out_weight, query_gain, key_gain,
            token_req, own_tokens, own_request,
        )
    col_count = reduced.shape[1]
    hidden_cols = lax.dynamic_slice_in_dim(hidden_f32, tp_index * col_count, col_count, 1)
    gate_cols = lax.dynamic_slice_in_dim(choose_row(mod_gate), tp_index * col_count, col_count)
    hidden_next = (hidden_cols + gate_cols[None, :] * reduced).astype(jnp.bfloat16)
    velocity = jnp.dot(hidden_next, final_weight, preferred_element_type=jnp.float32).astype(
        jnp.bfloat16
    )
    if lax.axis_size("tp") == 2:
        velocity = velocity.astype(jnp.float32) + lax.ppermute(
            velocity, "tp", [(0, 1), (1, 0)]
        ).astype(jnp.float32)
    else:
        velocity = lax.psum(velocity, "tp").astype(jnp.float32)
    step_delta = sigma_of(step_index + 1) - sigma_of(step_index)
    own_delta = jnp.sum(select * step_delta)
    latent_next = latent + own_delta * velocity
    token_live = own_tokens >= 0
    dec_input = jnp.where(token_live[:, None], latent_next, 0.0).astype(jnp.bfloat16)
    padded = with_halo(dec_input, (("seq", 0),), IMG_W)
    prev_owner = tile_owner[jnp.maximum(seq_index - 1, 0)]
    next_owner = tile_owner[jnp.minimum(seq_index + 1, seq_count - 1)]
    same_prev = (seq_index > 0) & (prev_owner == own_owner)
    same_next = (seq_index < seq_count - 1) & (next_owner == own_owner)
    upper = jnp.where(same_prev, padded[:IMG_W], 0.0)
    lower = jnp.where(same_next, padded[IMG_W + tile_rows :], 0.0)
    framed_tokens = jnp.concatenate([upper, padded[IMG_W : IMG_W + tile_rows], lower], axis=0)
    token_rows = tile_rows // IMG_W
    pixel_ch = LAT_CH // 4
    pixels = framed_tokens.reshape(token_rows + 2, IMG_W, pixel_ch, 2, 2)
    pixels = jnp.transpose(pixels, (0, 3, 1, 4, 2)).reshape(
        2 * (token_rows + 2), 2 * IMG_W, pixel_ch
    )
    framed = pixels[1 : 2 * token_rows + 3]
    framed = jnp.pad(framed, ((0, 0), (1, 1), (0, 0)))
    patches = jnp.concatenate(
        [
            framed[row_shift : row_shift + 2 * token_rows, col_shift : col_shift + 2 * IMG_W, :]
            for row_shift in range(3)
            for col_shift in range(3)
        ],
        axis=-1,
    )
    convolved = jnp.dot(
        patches.reshape(-1, 9 * pixel_ch), conv_weight, preferred_element_type=jnp.float32
    )
    pixel_live = jnp.broadcast_to(
        token_live.reshape(token_rows, 1, IMG_W, 1), (token_rows, 2, IMG_W, 2)
    ).reshape(-1)
    decoded = jnp.where(pixel_live[:, None], convolved, 0.0).astype(jnp.bfloat16)
    return (hidden_next, latent_next, decoded)


def solution(mesh):
    return jax.shard_map(
        shards,
        mesh=mesh,
        in_specs=(
            P("seq", None),
            P("seq", None),
            P("seq", "tp"),
            P("seq", "tp"),
            P(None, None, "tp"),
            P(None, None, "tp"),
            P("seq", "tp"),
            P("seq", "tp"),
            P("seq", "tp"),
            P("seq", "tp"),
            P(),
            P(),
            P(),
            P(),
            P(),
            P("tp", None),
            P(None, "tp"),
            P(),
            P(),
            P("seq", None),
            P(),
        ),
        out_specs=(P("seq", "tp"), P("seq", None), P("seq", "tp")),
        check_vma=False,
    )
```

```python
import math

import jax
import jax.numpy as jnp
from jax import lax
from jax.experimental import pallas as pl
from jax.experimental.pallas import tpu as pltpu
from jax.sharding import PartitionSpec as P

HD = 128
LAT_CH = 64
IMG_W = 64
STEPS = 8


EPSILON = 1e-06
SIGMA_SHIFT = 3.0


def with_halo(shard, sides, width):
    for axis, dim in sides:
        devices, length = (lax.axis_size(axis), shard.shape[dim])
        up = [(i, (i + 1) % devices) for i in range(devices - 1)]
        down = [(j, i) for i, j in up]
        last = lax.slice_in_dim(shard, length - width, length, axis=dim)
        first = lax.slice_in_dim(shard, 0, width, axis=dim)
        before = lax.ppermute(last, axis, up)
        after = lax.ppermute(first, axis, down)
        shard = jnp.concatenate([before, shard, after], axis=dim)
    return shard


def tile_layout(tile_owner, image_rows, tile_rows, row_width):
    request_count = image_rows.shape[0]
    tile_count = tile_owner.shape[0]
    earlier = jnp.sum((tile_owner[None, :] < tile_owner[:, None]).astype(jnp.int32), axis=1)
    ordinal = jnp.arange(tile_count, dtype=jnp.int32) - earlier
    mod_req = jnp.minimum(tile_owner, request_count - 1)
    picked = jnp.sum(
        jnp.where(
            mod_req[:, None] == jnp.arange(request_count, dtype=jnp.int32)[None, :],
            image_rows[None, :],
            0,
        ),
        axis=1,
    )
    live_rows = jnp.where(
        tile_owner < request_count,
        jnp.clip(picked * row_width - ordinal * tile_rows, 0, tile_rows),
        0,
    )
    return (mod_req, live_rows)


def sigma_of(step_index):
    fraction = 1.0 - step_index.astype(jnp.float32) / STEPS
    return SIGMA_SHIFT * fraction / (1.0 + (SIGMA_SHIFT - 1.0) * fraction)


def head_norm(projected, head_gain):
    row_count = projected.shape[0]
    shaped = projected.reshape(row_count, -1, HD)
    inverse = lax.rsqrt(jnp.mean(jnp.square(shaped), axis=2, keepdims=True) + EPSILON)
    return shaped * inverse * head_gain


def plain_branch(
    modulated, listed_rows, key_cache, value_cache, text_keys, text_values,
    query_weight, key_weight, value_weight, out_weight, query_gain, key_gain,
    token_req, own_tokens, own_request,
):
    tile_rows = modulated.shape[0]
    listed_x = modulated[listed_rows]
    local_width = key_cache.shape[1]
    local_heads = local_width // HD
    gathered_q, gathered_k, gathered_v, gathered_out = (
        lax.all_gather(query_weight, "seq", axis=0, tiled=True),
        lax.all_gather(key_weight, "seq", axis=0, tiled=True),
        lax.all_gather(value_weight, "seq", axis=0, tiled=True),
        lax.all_gather(out_weight, "seq", axis=0, tiled=True),
    )
    query_raw = jnp.dot(modulated, gathered_q, preferred_element_type=jnp.float32)
    key_raw = jnp.dot(listed_x, gathered_k, preferred_element_type=jnp.float32)
    value_raw = jnp.dot(listed_x, gathered_v, preferred_element_type=jnp.float32)
    queries = head_norm(query_raw, query_gain).astype(jnp.bfloat16)
    fresh_keys = head_norm(key_raw, key_gain).astype(jnp.bfloat16).reshape(-1, local_width)
    fresh_values = value_raw.astype(jnp.bfloat16)
    local_keys = key_cache.at[listed_rows].set(fresh_keys)
    local_values = value_cache.at[listed_rows].set(fresh_values)
    score_scale = 1.0 / math.sqrt(HD)
    text_key_tile = lax.dynamic_index_in_dim(text_keys, own_request, 0, keepdims=False).reshape(
        -1, local_heads, HD
    )
    text_value_tile = lax.dynamic_index_in_dim(text_values, own_request, 0, keepdims=False).reshape(
        -1, local_heads, HD
    )
    text_scores = (
        jnp.einsum("qhd,khd->hqk", queries, text_key_tile, preferred_element_type=jnp.float32)
        * score_scale
    )
    row_max = jnp.max(text_scores, axis=2)
    text_exp = jnp.exp(text_scores - row_max[..., None])
    row_sum = jnp.sum(text_exp, axis=2)
    weighted = jnp.einsum(
        "hqk,khd->hqd",
        text_exp.astype(jnp.bfloat16),
        text_value_tile,
        preferred_element_type=jnp.float32,
    )

    def attend(state_now, key_tile, value_tile, key_owner):
        old_max, old_sum, old_weighted = state_now
        allowed = (key_owner[None, :] == own_tokens[:, None]) & (own_tokens[:, None] >= 0)
        key_heads = key_tile.reshape(-1, local_heads, HD)
        value_heads = value_tile.reshape(-1, local_heads, HD)
        scores = (
            jnp.einsum("qhd,khd->hqk", queries, key_heads, preferred_element_type=jnp.float32)
            * score_scale
        )
        scores = jnp.where(allowed[None], scores, -jnp.inf)
        new_max = jnp.maximum(old_max, jnp.max(scores, axis=2))
        shrink = jnp.exp(old_max - new_max)
        exp_scores = jnp.exp(scores - new_max[..., None])
        new_sum = old_sum * shrink + jnp.sum(exp_scores, axis=2)
        new_weighted = old_weighted * shrink[..., None] + jnp.einsum(
            "hqk,khd->hqd",
            exp_scores.astype(jnp.bfloat16),
            value_heads,
            preferred_element_type=jnp.float32,
        )
        return (new_max, new_sum, new_weighted)

    pieces = (
        lax.all_gather(local_keys, "seq", axis=0, tiled=True),
        lax.all_gather(local_values, "seq", axis=0, tiled=True),
    )
    length = pieces[0].shape[0]
    key_owner = token_req
    key_block = 1024
    block_count = length // key_block
    stacked = (
        pieces[0].reshape(block_count, key_block, -1),
        pieces[1].reshape(block_count, key_block, -1),
        key_owner.reshape(block_count, key_block),
    )

    def scan_step(state_mid, blocks):
        return (attend(state_mid, blocks[0], blocks[1], blocks[2]), None)

    row_max, row_sum, weighted = lax.scan(scan_step, (row_max, row_sum, weighted), stacked)[0]
    attended = (
        jnp.transpose(weighted / row_sum[..., None], (1, 0, 2))
        .reshape(tile_rows, local_width)
        .astype(jnp.bfloat16)
    )
    partial_out = lax.dot_general(
        attended, gathered_out, (((1,), (1,)), ((), ())), preferred_element_type=jnp.float32
    )
    reduced = lax.psum_scatter(
        partial_out.astype(jnp.bfloat16), "tp", scatter_dimension=1, tiled=True
    ).astype(jnp.float32)
    return reduced


GROUP = 4


def group_size(seq_count, local_heads):
    if seq_count == GROUP * GROUP and seq_count == 2 * local_heads:
        return GROUP
    return 1


def attention_kernel(
    request_ref, place_ref, q_ref, k_ref, v_ref, tk_ref, tv_ref, key_req_ref, tok_req_ref, o_ref
):
    scale = 1.0 / math.sqrt(HD)
    q = q_ref[...]
    dims = (((1,), (1,)), ((), ()))
    s_text = lax.dot_general(q, tk_ref[0], dims, preferred_element_type=jnp.float32) * scale
    s_img = lax.dot_general(q, k_ref[...], dims, preferred_element_type=jnp.float32) * scale
    own = tok_req_ref[...]
    allowed = (key_req_ref[...] == own) & (own >= 0)
    s_img = jnp.where(allowed, s_img, -jnp.inf)
    top = jnp.maximum(
        jnp.max(s_text, axis=1, keepdims=True), jnp.max(s_img, axis=1, keepdims=True)
    )
    e_text = jnp.exp(s_text - top)
    e_img = jnp.exp(s_img - top)
    total = jnp.sum(e_text, axis=1, keepdims=True) + jnp.sum(e_img, axis=1, keepdims=True)
    acc = jnp.dot(e_text.astype(jnp.bfloat16), tv_ref[0], preferred_element_type=jnp.float32)
    acc += jnp.dot(e_img.astype(jnp.bfloat16), v_ref[...], preferred_element_type=jnp.float32)
    o_ref[...] = (acc / total).astype(jnp.bfloat16)


def attention(queries, keys, values, text_keys, text_values, requests, place, token_req, own_req):
    rows, width = queries.shape
    length = keys.shape[0]
    text = text_keys.shape[1]
    heads = width // HD
    tiles = requests.shape[0]
    tile_rows = rows // tiles
    grid_spec = pltpu.PrefetchScalarGridSpec(
        num_scalar_prefetch=2,
        grid=(heads, tiles),
        in_specs=[
            pl.BlockSpec((tile_rows, HD), lambda h, t, req, pos: (t, h)),
            pl.BlockSpec((length, HD), lambda h, t, req, pos: (0, h)),
            pl.BlockSpec((length, HD), lambda h, t, req, pos: (0, h)),
            pl.BlockSpec((1, text, HD), lambda h, t, req, pos: (req[t], 0, pos[0] * heads + h)),
            pl.BlockSpec((1, text, HD), lambda h, t, req, pos: (req[t], 0, pos[0] * heads + h)),
            pl.BlockSpec((1, length), lambda h, t, req, pos: (0, 0)),
            pl.BlockSpec((tile_rows, 1), lambda h, t, req, pos: (t, 0)),
        ],
        out_specs=pl.BlockSpec((tile_rows, HD), lambda h, t, req, pos: (t, h)),
    )
    return pl.pallas_call(
        attention_kernel,
        grid_spec=grid_spec,
        out_shape=jax.ShapeDtypeStruct((rows, width), jnp.bfloat16),
        compiler_params=pltpu.CompilerParams(vmem_limit_bytes=32 * 1024 * 1024),
        cost_estimate=pl.CostEstimate(
            flops=4 * rows * width * (length + text),
            bytes_accessed=8 * length * width,
            transcendentals=rows * heads * (length + text),
        ),
    )(
        requests, place, queries, keys, values, text_keys, text_values,
        token_req.reshape(1, -1), own_req.reshape(-1, 1),
    )


def interleave(first, second):
    rows = first.shape[0]
    both = jnp.stack([first.reshape(rows, -1, HD), second.reshape(rows, -1, HD)], axis=2)
    return both.reshape(rows, -1)


def grouped_branch(
    group, modulated, listed_rows, key_cache, value_cache, text_keys, text_values,
    query_weight, key_weight, value_weight, out_weight, query_gain, key_gain,
    token_req, mod_req,
):
    tile_rows, model = modulated.shape
    seq_count = lax.axis_size("seq")
    tp_count = lax.axis_size("tp")
    seq_index = lax.axis_index("seq")
    tp_index = lax.axis_index("tp")
    lines = seq_count // group
    place = lax.rem(seq_index, group)
    line = seq_index // group
    core = lax.rem(seq_index, 2)
    side = place // 2
    width = key_cache.shape[1] // group
    depth = query_weight.shape[0]
    half_rows = group * tile_rows // 2
    inner = [[z * group + p for p in range(group)] for z in range(lines)]
    turns = [
        [(z * group + p, p * group + (z + k) % group) for z in range(lines) for p in range(group)]
        for k in range(group)
    ]

    def line_gather(block):
        full = jnp.zeros((lines,) + block.shape, block.dtype)
        for k in range(lines):
            got = block
            if k > 0:
                got = lax.ppermute(
                    block, "seq", [(i, (i + k * group) % seq_count) for i in range(seq_count)]
                )
            full = lax.dynamic_update_slice(
                full, got[None], (lax.rem(line + lines - k, lines), jnp.int32(0), jnp.int32(0))
            )
        return full.reshape(-1, block.shape[1])

    def paired(block, flip, position):
        got = lax.ppermute(block, "seq", [(i, i ^ flip) for i in range(seq_count)])
        first = jnp.where(position == 0, block, got)
        second = jnp.where(position == 0, got, block)
        return jnp.concatenate([first, second], axis=0)

    def plane_gather(block):
        return paired(paired(block, 2, side), 1, core)

    def spot_of(at):
        return lax.rem(at, 2) * 2 + at // 2

    def tile_order(rows):
        shaped = rows.reshape((2, 2, lines, -1) + rows.shape[1:])
        return jnp.swapaxes(shaped, 0, 2).reshape((seq_count, -1) + rows.shape[1:])

    moved = jnp.concatenate(
        [interleave(key_weight, value_weight), interleave(key_cache, value_cache)], axis=0
    )
    moved = lax.all_to_all(moved, "seq", split_axis=1, concat_axis=0, tiled=True)
    moved = moved.reshape(seq_count, -1, HD)
    head_weight = moved[:, :depth].reshape(-1, HD)
    head_cache = moved[:, depth:]

    listed_x = jnp.concatenate(
        [
            modulated[listed_rows],
            jnp.broadcast_to(listed_rows[:, None], (listed_rows.shape[0], HD)).astype(
                jnp.bfloat16
            ),
        ],
        axis=1,
    )
    all_listed = plane_gather(line_gather(listed_x))
    lined = lax.all_to_all(
        line_gather(query_weight).reshape(lines, depth, group * width), "seq",
        split_axis=2, concat_axis=1, axis_index_groups=inner, tiled=True,
    )
    query_w = lined.reshape(model, width)
    tokens = plane_gather(modulated)
    fresh_raw = jnp.dot(all_listed[:, :model], head_weight, preferred_element_type=jnp.float32)
    fresh_keys = head_norm(fresh_raw, key_gain).reshape(-1, HD)
    fresh = jnp.where(core == 0, fresh_keys, fresh_raw).astype(jnp.bfloat16)
    fresh = tile_order(fresh)
    spots = tile_order(all_listed[:, model].astype(jnp.int32))[:, None, :]
    onehot = spots == jnp.arange(tile_rows, dtype=jnp.int32)[None, :, None]
    placed = jnp.einsum(
        "trl,tld->trd", onehot.astype(jnp.bfloat16), fresh, preferred_element_type=jnp.float32
    ).astype(jnp.bfloat16)
    mine = jnp.where(jnp.any(onehot, axis=2, keepdims=True), placed, head_cache)
    mine = mine.reshape(-1, HD)
    other = lax.ppermute(mine, "seq", [(i, i ^ 1) for i in range(seq_count)])
    keys = jnp.where(core == 0, mine, other)
    values = jnp.where(core == 0, other, mine)

    query_raw = jnp.dot(tokens, query_w, preferred_element_type=jnp.float32)
    queries = head_norm(query_raw, query_gain).astype(jnp.bfloat16).reshape(-1, width)
    got_queries, got_requests, got_tokens = [], [], []
    for k in range(group):
        target = lax.rem(line + k, group)
        block = lax.dynamic_slice(
            queries, (lax.rem(target, 2) * half_rows, (target // 2) * HD), (half_rows, HD)
        )
        got_queries.append(lax.ppermute(block, "seq", turns[k]))
        for half in range(2):
            tile = lax.rem(place + group - k, group) * group + core + 2 * half
            got_requests.append(lax.dynamic_slice_in_dim(mod_req, tile, 1))
            got_tokens.append(lax.dynamic_slice_in_dim(token_req, tile * tile_rows, tile_rows))
    out_w = line_gather(lax.optimization_barrier((out_weight, moved))[0])
    attended = attention(
        jnp.concatenate(got_queries, axis=0), keys, values, text_keys, text_values,
        jnp.concatenate(got_requests), (seq_index // 2).reshape(1),
        token_req, jnp.concatenate(got_tokens),
    )
    own_heads = jnp.zeros((2 * half_rows, width), jnp.bfloat16)
    for k in range(group):
        block = attended[k * half_rows : (k + 1) * half_rows]
        back = lax.ppermute(block, "seq", [(j, i) for i, j in turns[k]])
        origin = lax.rem(line + k, group)
        own_heads = lax.dynamic_update_slice(
            own_heads, back, (lax.rem(origin, 2) * half_rows, (origin // 2) * HD)
        )
    all_heads = jnp.zeros((2 * half_rows, group * width), jnp.bfloat16)
    for k in range(group):
        got = own_heads
        if k > 0:
            got = lax.ppermute(own_heads, "seq", [(i, i ^ k) for i in range(seq_count)])
        all_heads = lax.dynamic_update_slice(
            all_heads, got, (jnp.int32(0), jnp.bitwise_xor(place, k) * width)
        )
    partial_out = lax.dot_general(
        all_heads, out_w, (((1,), (1,)), ((), ())), preferred_element_type=jnp.float32
    ).astype(jnp.bfloat16)
    share = partial_out.shape[1] // tp_count
    pieces = jnp.zeros((group, tile_rows, share), jnp.float32)
    for k in range(group):
        peer = jnp.bitwise_xor(place, k)
        total = 0.0
        for j in range(tp_count):
            block = lax.dynamic_slice(
                partial_out,
                (spot_of(peer) * tile_rows, lax.rem(tp_index + j, tp_count) * share),
                (tile_rows, share),
            )
            if k > 0 or j > 0:
                block = lax.ppermute(
                    block,
                    ("seq", "tp"),
                    [
                        (i * tp_count + t, (i ^ k) * tp_count + (t + j) % tp_count)
                        for i in range(seq_count)
                        for t in range(tp_count)
                    ],
                )
            total = total + block.astype(jnp.float32)
        pieces = lax.dynamic_update_slice(pieces, total[None], (peer, jnp.int32(0), jnp.int32(0)))
    pieces = pieces.reshape(group, tile_rows, -1, depth)
    return jnp.transpose(pieces, (1, 2, 0, 3)).reshape(tile_rows, -1)


def shards(
    hidden,
    latent,
    key_cache,
    value_cache,
    text_keys,
    text_values,
    query_weight,
    key_weight,
    value_weight,
    out_weight,
    query_gain,
    key_gain,
    mod_shift,
    mod_scale,
    mod_gate,
    final_weight,
    conv_weight,
    image_rows,
    tile_owner,
    listed,
    step_index,
):
    tile_rows = hidden.shape[0]
    seq_count = lax.axis_size("seq")
    seq_index = lax.axis_index("seq")
    tp_index = lax.axis_index("tp")
    request_count = image_rows.shape[0]
    mod_req, live_rows = tile_layout(tile_owner, image_rows, tile_rows, IMG_W)
    row_index = jnp.arange(tile_rows, dtype=jnp.int32)
    token_req = jnp.where(row_index[None, :] < live_rows[:, None], tile_owner[:, None], -1).reshape(
        -1
    )
    own_tokens = lax.dynamic_slice_in_dim(token_req, seq_index * tile_rows, tile_rows)
    own_request = mod_req[seq_index]
    own_owner = tile_owner[seq_index]
    select = (jnp.arange(request_count, dtype=jnp.int32) == own_request).astype(jnp.float32)

    def choose_row(table):
        return jnp.dot(select, table, precision=lax.Precision.HIGHEST)

    hidden_f32 = hidden.astype(jnp.float32)
    row_mean = jnp.mean(hidden_f32, axis=1, keepdims=True)
    row_var = jnp.mean(jnp.square(hidden_f32 - row_mean), axis=1, keepdims=True)
    normed = (hidden_f32 - row_mean) * lax.rsqrt(row_var + EPSILON)
    modulated = (
        (1.0 + choose_row(mod_scale))[None, :] * normed + choose_row(mod_shift)[None, :]
    ).astype(jnp.bfloat16)
    local_width = key_cache.shape[1]
    group = group_size(seq_count, local_width // HD)
    if group > 1:
        reduced = grouped_branch(
            group, modulated, listed[0], key_cache, value_cache, text_keys, text_values,
            query_weight, key_weight, value_weight, out_weight, query_gain, key_gain,
            token_req, mod_req,
        )
    else:
        reduced = plain_branch(
            modulated, listed[0], key_cache, value_cache, text_keys, text_values,
            query_weight, key_weight, value_weight, out_weight, query_gain, key_gain,
            token_req, own_tokens, own_request,
        )
    col_count = reduced.shape[1]
    hidden_cols = lax.dynamic_slice_in_dim(hidden_f32, tp_index * col_count, col_count, 1)
    gate_cols = lax.dynamic_slice_in_dim(choose_row(mod_gate), tp_index * col_count, col_count)
    hidden_next = (hidden_cols + gate_cols[None, :] * reduced).astype(jnp.bfloat16)
    velocity = jnp.dot(hidden_next, final_weight, preferred_element_type=jnp.float32).astype(
        jnp.bfloat16
    )
    if lax.axis_size("tp") == 2:
        velocity = velocity.astype(jnp.float32) + lax.ppermute(
            velocity, "tp", [(0, 1), (1, 0)]
        ).astype(jnp.float32)
    else:
        velocity = lax.psum(velocity, "tp").astype(jnp.float32)
    step_delta = sigma_of(step_index + 1) - sigma_of(step_index)
    own_delta = jnp.sum(select * step_delta)
    latent_next = latent + own_delta * velocity
    token_live = own_tokens >= 0
    dec_input = jnp.where(token_live[:, None], latent_next, 0.0).astype(jnp.bfloat16)
    padded = with_halo(dec_input, (("seq", 0),), IMG_W)
    prev_owner = tile_owner[jnp.maximum(seq_index - 1, 0)]
    next_owner = tile_owner[jnp.minimum(seq_index + 1, seq_count - 1)]
    same_prev = (seq_index > 0) & (prev_owner == own_owner)
    same_next = (seq_index < seq_count - 1) & (next_owner == own_owner)
    upper = jnp.where(same_prev, padded[:IMG_W], 0.0)
    lower = jnp.where(same_next, padded[IMG_W + tile_rows :], 0.0)
    framed_tokens = jnp.concatenate([upper, padded[IMG_W : IMG_W + tile_rows], lower], axis=0)
    token_rows = tile_rows // IMG_W
    pixel_ch = LAT_CH // 4
    pixels = framed_tokens.reshape(token_rows + 2, IMG_W, pixel_ch, 2, 2)
    pixels = jnp.transpose(pixels, (0, 3, 1, 4, 2)).reshape(
        2 * (token_rows + 2), 2 * IMG_W, pixel_ch
    )
    framed = pixels[1 : 2 * token_rows + 3]
    framed = jnp.pad(framed, ((0, 0), (1, 1), (0, 0)))
    patches = jnp.concatenate(
        [
            framed[row_shift : row_shift + 2 * token_rows, col_shift : col_shift + 2 * IMG_W, :]
            for row_shift in range(3)
            for col_shift in range(3)
        ],
        axis=-1,
    )
    convolved = jnp.dot(
        patches.reshape(-1, 9 * pixel_ch), conv_weight, preferred_element_type=jnp.float32
    )
    pixel_live = jnp.broadcast_to(
        token_live.reshape(token_rows, 1, IMG_W, 1), (token_rows, 2, IMG_W, 2)
    ).reshape(-1)
    decoded = jnp.where(pixel_live[:, None], convolved, 0.0).astype(jnp.bfloat16)
    return (hidden_next, latent_next, decoded)


def solution(mesh):
    return jax.shard_map(
        shards,
        mesh=mesh,
        in_specs=(
            P("seq", None),
            P("seq", None),
            P("seq", "tp"),
            P("seq", "tp"),
            P(None, None, "tp"),
            P(None, None, "tp"),
            P("seq", "tp"),
            P("seq", "tp"),
            P("seq", "tp"),
            P("seq", "tp"),
            P(),
            P(),
            P(),
            P(),
            P(),
            P("tp", None),
            P(None, "tp"),
            P(),
            P(),
            P("seq", None),
            P(),
        ),
        out_specs=(P("seq", "tp"), P("seq", None), P("seq", "tp")),
        check_vma=False,
    )
```
